256 devices in a mesh: row: 32 (over x, z), col: 8 (over y, core).
Axes of the slice: x: 4, y: 4, z: 8, core: 2. Of those that a mesh axis runs over, the one named last changes fastest.
Arguments:
- features: bfloat16 [16384, 512], P(('row', 'col')), may hold values from -0.5 to 0.5
- slot_of_ray: int32 [16384], P(('row', 'col')), may hold values from 0 to 63
- noise: float32 [16384], P(('row', 'col')), may hold values from 0.2 to 1
Outputs:
- front: float32 [16384, 8, 2048], P('row', 'col')
- factor: float32 [16384, 1024], P('row')
The draws below stay inside these ranges and needn't reach their ends.
All inputs are finite; a program needn't handle non-finite values.
Results may differ from the reference program's by a relative error of at most 0.0003.
Values may be sent and summed in bfloat16 or wider, within the bound.
A program may use at most 64 MiB of HBM per device.

```python
import math
import jax
import jax.numpy as jnp
from jax import lax

RAY_DEV = 64
F = 512
PANEL = 256
PANELS = 4
NT = 64
RAYS = 16384
N_ROW = 32
N_COL = 8


def touch_ends(entries, own_key, low, largest):
    longest = entries.shape.index(max(entries.shape))
    spots = []
    for shift in (0, 1):
        where = [jax.random.randint(jax.random.fold_in(own_key, axis), (), 0, length) for axis, length in enumerate(entries.shape)]
        where[longest] = (where[longest] + shift) % entries.shape[longest]
        spots.append(tuple(where))
    return entries.at[spots[0]].set(low).at[spots[1]].set(largest)


def block_levels(rng, dims, shards, smallest, high):
    def one(axis_at, parts):
        steps = jax.random.uniform(jax.random.fold_in(jax.random.fold_in(rng, 6), axis_at), (parts,), jnp.float32, smallest / len(shards), high / len(shards))
        return jnp.repeat(jnp.exp(steps), dims[axis_at] // parts).reshape((-1,) + (1,) * (len(dims) - axis_at - 1))

    factor_of = one(*shards[0])
    for cut in shards[1:]:
        factor_of = factor_of * one(*cut)
    return factor_of


def normal_values(rng, shape, scale, limit, cuts=(), kind=jnp.bfloat16):
    factor_of = block_levels(rng, shape, cuts, -0.22, 0.18) if cuts else 1.0
    values = jax.random.normal(rng, shape, jnp.float32) * scale * factor_of
    return jnp.minimum(jnp.maximum(values, -limit), limit).astype(kind)


def setup_inputs(seed: int = 0) -> dict:
    key_list = jax.random.split(jax.random.key(seed), 4)
    return {
        "features": normal_values(key_list[0], (RAYS, F), (F // 4) ** -0.5, 0.5, ((0, 256),)),
        "slot_of_ray": touch_ends(jax.random.randint(key_list[1], (RAYS,), 0, NT), jax.random.fold_in(key_list[1], 1), 0, NT - 1).astype(jnp.int32),
        "noise": jnp.clip(jnp.exp(math.log(1.0) - 1.609438 * jax.random.uniform(key_list[2], (RAYS,), jnp.float32) ** block_levels(key_list[2], (RAYS,), ((0, 256),), -0.2, 0.2)), 0.2, 1.0),
    }


def time_rate():
    length = NT / 8.0
    return 1.0 / (2.0 * length * length)

def reference(features, slot_of_ray, noise):
    slot_values = slot_of_ray.astype(jnp.float32)
    gram_tile = lax.dot_general(features.astype(jnp.float32), features.astype(jnp.float32), (((1,), (1,)), ((), ())), preferred_element_type=jnp.float32)
    slot_gap = slot_values[:, None] - slot_values[None, :]
    complement = gram_tile * jnp.exp(-slot_gap * slot_gap * time_rate())
    ray_rows = jnp.arange(RAYS, dtype=jnp.int32)
    complement = complement.at[ray_rows, ray_rows].add(noise)
    columns = []
    for panel_number in range(PANELS):
        panel_start = panel_number * PANEL
        panel_top = complement[panel_start:panel_start + PANEL]
        triangle = jnp.linalg.cholesky(panel_top[:, panel_start:panel_start + PANEL])
        solved = jax.scipy.linalg.solve_triangular(triangle, panel_top, lower=True)
        complement = complement - lax.dot_general(solved.astype(jnp.float32), solved.astype(jnp.float32), (((0,), (0,)), ((), ())), precision=lax.Precision.HIGHEST, preferred_element_type=jnp.float32)
        below_mask = ray_rows[:, None] >= panel_start + jnp.arange(PANEL, dtype=jnp.int32)[None, :]
        columns.append(jnp.where(below_mask, solved.T, 0.0))
    factor = jnp.concatenate(columns, axis=1)
    eliminated = PANELS * PANEL
    remaining = (ray_rows[:, None] >= eliminated) & (ray_rows[None, :] >= eliminated)
    front_out = jnp.where(remaining, complement, 0.0)
    front_out = front_out.reshape(RAYS, N_ROW, N_COL, RAY_DEV).transpose(0, 2, 1, 3).reshape(RAYS, N_COL, N_ROW * RAY_DEV)
    return (front_out, factor)
```

```python
import functools

import jax
import jax.numpy as jnp
from jax import lax
from jax.experimental import pallas as pl
from jax.experimental.pallas import tpu as pltpu
from jax.sharding import PartitionSpec as P

PANEL = 256
PANELS = 4
NT = 64
HEAD = PANEL * PANELS
EXTRA = 128
W = 8
B = 128
MESH = pl.DeviceIdType.MESH
HIGHEST = lax.Precision.HIGHEST
F32 = jnp.float32
BF16 = jnp.bfloat16
VMEM = pl.BlockSpec(memory_space=pltpu.VMEM)
ANY = pl.BlockSpec(memory_space=pl.ANY)


def time_rate():
    length = NT / 8.0
    return 1.0 / (2.0 * length * length)


def nn(a, b, precision=None):
    return lax.dot_general(a, b, (((1,), (0,)), ((), ())), precision=precision, preferred_element_type=F32)


def nt(a, b, precision=None):
    return lax.dot_general(a, b, (((1,), (1,)), ((), ())), precision=precision, preferred_element_type=F32)


def tn(a, b, precision=None):
    return lax.dot_general(a, b, (((0,), (0,)), ((), ())), precision=precision, preferred_element_type=F32)


def split(x):
    hi = x.astype(BF16)
    return hi, (x - hi.astype(F32)).astype(BF16)


def gather_kernel(n_row, n_col, pay_ref, col_ref, row_ref, head_ref, local_sem, csend, crecv, rsend, rrecv, hsend, hrecv):
    r, c = lax.axis_index("row"), lax.axis_index("col")
    rays = pay_ref.shape[0]

    barrier = pltpu.get_barrier_semaphore()
    for d in range(1, n_row):
        pl.semaphore_signal(barrier, inc=1, device_id=(lax.rem(r + d, n_row), c), device_id_type=MESH)
    for d in range(1, n_col):
        pl.semaphore_signal(barrier, inc=1, device_id=(r, lax.rem(c + d, n_col)), device_id_type=MESH)
    pl.semaphore_wait(barrier, n_row + n_col - 2)

    def to_rows(d, src_row):
        return pltpu.make_async_remote_copy(
            src_ref=pay_ref,
            dst_ref=col_ref.at[src_row],
            send_sem=csend.at[d],
            recv_sem=crecv.at[src_row],
            device_id=(lax.rem(r + d, n_row), c),
            device_id_type=MESH,
        )

    def to_cols(d, src_col):
        return pltpu.make_async_remote_copy(
            src_ref=pay_ref,
            dst_ref=row_ref.at[src_col],
            send_sem=rsend.at[d],
            recv_sem=rrecv.at[src_col],
            device_id=(r, lax.rem(c + d, n_col)),
            device_id_type=MESH,
        )

    def head_to_cols(d, src_col):
        return pltpu.make_async_remote_copy(
            src_ref=col_ref.at[pl.ds(0, 2)],
            dst_ref=head_ref.at[:, pl.ds(pl.multiple_of(src_col * rays, rays), rays)],
            send_sem=hsend.at[d],
            recv_sem=hrecv.at[src_col],
            device_id=(r, lax.rem(c + d, n_col)),
            device_id_type=MESH,
        )

    @pl.when(r < 2)
    def _():
        for d in range(1, n_row):
            to_rows(d, r).start()

    own = pltpu.make_async_copy(pay_ref, col_ref.at[r], local_sem.at[0])
    own.start()
    own_row = pltpu.make_async_copy(pay_ref, row_ref.at[c], local_sem.at[1])
    own_row.start()
    own.wait()
    for s in range(2):
        @pl.when(r != s)
        def _(s=s):
            to_rows(1, s).wait_recv()

    for d in range(1, n_col):
        head_to_cols(d, c).start()
    own_head = pltpu.make_async_copy(
        col_ref.at[pl.ds(0, 2)], head_ref.at[:, pl.ds(pl.multiple_of(c * rays, rays), rays)], local_sem.at[2]
    )
    own_head.start()

    @pl.when(r >= 2)
    def _():
        for d in range(1, n_row):
            to_rows(d, r).start()

    for d in range(1, n_col):
        to_cols(d, c).start()

    own_row.wait()
    own_head.wait()
    for d in range(1, n_col):
        head_to_cols(d, lax.rem(c + d, n_col)).wait_recv()
        to_cols(d, lax.rem(c + d, n_col)).wait_recv()
    for s in range(2, n_row):
        @pl.when(r != s)
        def _(s=s):
            to_rows(1, s).wait_recv()
    for d in range(1, n_col):
        head_to_cols(d, c).wait_send()
        to_cols(d, c).wait_send()
    for d in range(1, n_row):
        to_rows(d, r).wait_send()


def gather(payload, n_row, n_col):
    rays, width = payload.shape
    dma = pltpu.SemaphoreType.DMA
    return pl.pallas_call(
        functools.partial(gather_kernel, n_row, n_col),
        out_shape=(
            jax.ShapeDtypeStruct((n_row, rays, width), BF16),
            jax.ShapeDtypeStruct((n_col, rays, width), BF16),
            jax.ShapeDtypeStruct((2, n_col * rays, width), BF16),
        ),
        in_specs=[ANY],
        out_specs=(ANY, ANY, ANY),
        scratch_shapes=[
            dma((3,)), dma((n_row,)), dma((n_row,)), dma((n_col,)), dma((n_col,)), dma((n_col,)), dma((n_col,)),
        ],
        compiler_params=pltpu.CompilerParams(collective_id=0, has_side_effects=True),
        name="gather_features",
    )(payload)


def table():
    s = lax.broadcasted_iota(jnp.int32, (EXTRA, 512), 0)
    q = lax.broadcasted_iota(jnp.int32, (EXTRA, 512), 1)
    part = q // NT
    gap = (s - q % NT).astype(F32)
    value = jnp.exp(-gap * gap * time_rate())
    hi = value.astype(BF16).astype(F32)
    mid = (value - hi).astype(BF16).astype(F32)
    low = value - hi - mid
    kernel_part = jnp.where(part == 0, hi, jnp.where(part == 1, mid, jnp.where(part == 2, low, 0.0)))
    chosen = jnp.where(part < 4, kernel_part, jnp.where(gap == 0.0, 1.0, 0.0))
    return jnp.where(s < NT, chosen, 0.0).astype(BF16)


def lookups(extra, tab):
    both = nn(extra, tab).astype(BF16)
    return both[:, :256], both[:, 256:]


def noise_of(extra):
    e = extra[:, NT : NT + 3].astype(F32)
    return (e[:, 0:1] + e[:, 1:2]) + e[:, 2:3]


def factor_block(d_ref):
    lane = lax.broadcasted_iota(jnp.int32, (W, B), 1)
    sub = lax.broadcasted_iota(jnp.int32, (W, B), 0)

    def row(x, i):
        return jnp.broadcast_to(x[i : i + 1, :], (W, B))

    def col(x, i):
        return jnp.broadcast_to(x[:, i : i + 1], (W, B))

    for k in range(B // W):
        lo = W * k
        rows = d_ref[lo : lo + W, :]
        cols = [col(rows, lo + i) for i in range(W)]
        inside = (lane >= lo) & (lane < lo + W)
        rows = jnp.where(inside, jnp.where(lane - lo == sub, 1.0, 0.0), rows)
        done = jnp.zeros((W, B), F32)
        for i in range(W):
            pivot = row(cols[i], i)
            inverse = 1.0 / pivot
            current = row(rows, i)
            done = jnp.where(sub == i, current * lax.rsqrt(pivot), done)
            scaled = current * inverse
            rows = jnp.where(sub == i, scaled, rows - cols[i] * scaled)
            for j in range(i + 1, W):
                entry = row(cols[j], i) * inverse
                cols[j] = jnp.where(sub == i, entry, cols[j] - cols[i] * entry)
        d_ref[lo : lo + W, :] = done
        spread = [row(rows, i) for i in range(W)]
        for m in range(k + 1, B // W):
            other = d_ref[W * m : W * m + W, :]
            total = jnp.where(inside, 0.0, other)
            for i in range(W):
                total = total - col(other, lo + i) * spread[i]
            d_ref[W * m : W * m + W, :] = total


def head_kernel(head_ref, uhi_ref, ulo_ref, whi_ref, wlo_ref, s_ref, w_ref, d_ref):
    n = HEAD // B
    feat = head_ref[:, : head_ref.shape[1] - EXTRA]
    extra = head_ref[:, head_ref.shape[1] - EXTRA :]
    value, hot = lookups(extra, table())
    noise = noise_of(extra)
    for i in range(n):
        rs = slice(B * i, B * i + B)
        rr = lax.broadcasted_iota(jnp.int32, (B, HEAD - B * i), 0)
        cc = lax.broadcasted_iota(jnp.int32, (B, HEAD - B * i), 1)
        s_ref[rs, B * i :] = nt(feat[rs], feat[B * i :]) * nt(value[rs], hot[B * i :]) + jnp.where(rr == cc, noise[rs], 0.0)

    r = lax.broadcasted_iota(jnp.int32, (B, B), 0)
    c = lax.broadcasted_iota(jnp.int32, (B, B), 1)

    def tail(j):
        def go():
            lo = B * (j + 1)
            if lo >= HEAD:
                return
            solved = nn(w_ref[j], s_ref[lo - B : lo, lo:], HIGHEST)
            s_ref[lo - B : lo, lo:] = solved
            uhi_ref[lo - B : lo, lo:], ulo_ref[lo - B : lo, lo:] = split(solved)
            for i in range(j + 1, n):
                at = B * (i - j - 1)
                s_ref[B * i : B * i + B, B * i :] -= tn(solved[:, at : at + B], solved[:, at:], HIGHEST)

        return go

    def step(j, carry):
        at = pl.multiple_of(j * B, B)
        d_ref[...] = s_ref[pl.ds(at, B), pl.ds(at, B)]
        factor_block(d_ref)
        w_ref[j] = jnp.where(r >= c, d_ref[...], 0.0)
        lax.switch(j, [tail(i) for i in range(n)])
        return carry

    lax.fori_loop(0, n, step, 0)
    for p in range(PANELS):
        a, b = w_ref[2 * p], w_ref[2 * p + 1]
        low = -nn(b, tn(s_ref[PANEL * p : PANEL * p + B, PANEL * p + B : PANEL * p + PANEL], a, HIGHEST), HIGHEST)
        for x, rs, cs in ((a, slice(0, B), slice(0, B)), (low, slice(B, PANEL), slice(0, B)), (b, slice(B, PANEL), slice(B, PANEL))):
            whi_ref[p, rs, cs], wlo_ref[p, rs, cs] = split(x)
        whi_ref[p, :B, B:] = jnp.zeros((B, B), BF16)
        wlo_ref[p, :B, B:] = jnp.zeros((B, B), BF16)


def factor_head(head):
    return pl.pallas_call(
        head_kernel,
        out_shape=(
            jax.ShapeDtypeStruct((HEAD, HEAD), BF16),
            jax.ShapeDtypeStruct((HEAD, HEAD), BF16),
            jax.ShapeDtypeStruct((PANELS, PANEL, PANEL), BF16),
            jax.ShapeDtypeStruct((PANELS, PANEL, PANEL), BF16),
        ),
        in_specs=[VMEM],
        out_specs=(VMEM,) * 4,
        scratch_shapes=[pltpu.VMEM((HEAD, HEAD), F32), pltpu.VMEM((HEAD // B, B, B), F32), pltpu.VMEM((B, B), F32)],
        compiler_params=pltpu.CompilerParams(vmem_limit_bytes=40 << 20),
        name="factor_head",
    )(head)


def front_kernel(row_ref, head_ref, col_ref, uhi_ref, ulo_ref, whi_ref, wlo_ref, front_ref, factor_ref, tab_ref, hhot_ref, rval_ref, rhi_ref, rlo_ref, hi_ref, lo_ref):
    step = pl.program_id(0)
    r, c = lax.axis_index("row"), lax.axis_index("col")
    f = head_ref.shape[1] - EXTRA
    rows = row_ref.shape[0]
    tile = col_ref.shape[0]
    rays = rows // lax.axis_size("col")

    def solve(ref, value, noise, hi_out, lo_out):
        feat = ref[:, :f]
        n = ref.shape[0]
        for p in range(PANELS):
            ps = slice(PANEL * p, PANEL * p + PANEL)
            x = nt(feat, head_ref[ps, :f]) * nt(value, hhot_ref[ps])
            if noise is not None:
                rr = r * n + lax.broadcasted_iota(jnp.int32, (n, PANEL), 0)
                cc = PANEL * p + lax.broadcasted_iota(jnp.int32, (n, PANEL), 1)
                x = x + jnp.where(rr == cc, noise, 0.0)
            if p > 0:
                k = PANEL * p
                x = x - (nn(hi_out[:, :k], uhi_ref[:k, ps]) + (nn(hi_out[:, :k], ulo_ref[:k, ps]) + nn(lo_out[:, :k], uhi_ref[:k, ps])))
            xh, xl = split(x)
            s = nt(xh, whi_ref[p]) + (nt(xh, wlo_ref[p]) + nt(xl, whi_ref[p]))
            hi_out[:, ps], lo_out[:, ps] = split(s)
            if noise is not None:
                factor_ref[:, ps] = jnp.where(rr >= cc, s, 0.0)

    @pl.when(step == 0)
    def _():
        tab_ref[...] = table()
        hhot_ref[...] = lookups(head_ref[:, f:], tab_ref[...])[1]
        rval_ref[...] = lookups(row_ref[:, f:], tab_ref[...])[0]
        solve(row_ref, rval_ref[...], noise_of(row_ref[:, f:]), rhi_ref, rlo_ref)

    value, hot = lookups(col_ref[:, f:], tab_ref[...])
    solve(col_ref, value, None, hi_ref, lo_ref)
    full = nt(row_ref[:, :f], col_ref[:, :f]) * nt(rval_ref[...], hot)
    ri = lax.broadcasted_iota(jnp.int32, (rows, tile), 0)
    li = step * tile + lax.broadcasted_iota(jnp.int32, (rows, tile), 1)
    col_local = li - r * rays
    full = full + jnp.where(ri - c * rays == col_local, jnp.where((col_local >= 0) & (col_local < rays), noise_of(row_ref[:, f:]), 0.0), 0.0)
    full = full - (nt(rhi_ref[...], hi_ref[...]) + (nt(rhi_ref[...], lo_ref[...]) + nt(rlo_ref[...], hi_ref[...])))
    first = jnp.where(r >= HEAD // rows, HEAD // (rows // rays * rays) * rays, tile * pl.num_programs(0))
    front_ref[:, 0, :] = jnp.where(li >= first, full, 0.0)


def front_and_factor(row, head, col, uhi, ulo, whi, wlo):
    rows, width = row.shape
    cols = col.shape[0]
    tile = 512
    whole = lambda a: pl.BlockSpec(a.shape, lambda i: (0,) * a.ndim)
    return pl.pallas_call(
        front_kernel,
        grid=(cols // tile,),
        out_shape=(jax.ShapeDtypeStruct((rows, 1, cols), F32), jax.ShapeDtypeStruct((rows, HEAD), F32)),
        in_specs=[whole(row), whole(head), pl.BlockSpec((tile, width), lambda i: (i, 0)), whole(uhi), whole(ulo), whole(whi), whole(wlo)],
        out_specs=(pl.BlockSpec((rows, 1, tile), lambda i: (0, 0, i)), pl.BlockSpec((rows, HEAD), lambda i: (0, 0))),
        scratch_shapes=[
            pltpu.VMEM((EXTRA, 512), BF16),
            pltpu.VMEM((HEAD, 256), BF16),
            pltpu.VMEM((rows, 256), BF16),
            pltpu.VMEM((rows, HEAD), BF16),
            pltpu.VMEM((rows, HEAD), BF16),
            pltpu.VMEM((tile, HEAD), BF16),
            pltpu.VMEM((tile, HEAD), BF16),
        ],
        compiler_params=pltpu.CompilerParams(vmem_limit_bytes=56 << 20),
        name="front_and_factor",
    )(row, head, col, uhi, ulo, whi, wlo)


def shards(features, slot_of_ray, noise):
    n_row, n_col = lax.axis_size("row"), lax.axis_size("col")
    rays = noise.shape[0]
    lanes = jnp.arange(EXTRA, dtype=jnp.int32)[None, :]
    hi = noise.astype(BF16).astype(F32)
    mid = (noise - hi).astype(BF16).astype(F32)
    low = noise - hi - mid
    extra = jnp.where(lanes == slot_of_ray[:, None], 1.0, 0.0)
    for i, part in enumerate((hi, mid, low)):
        extra = jnp.where(lanes == NT + i, part[:, None], extra)
    payload = jnp.concatenate([features, extra.astype(BF16)], axis=1)
    width = payload.shape[1]
    col, row, head = gather(payload, n_row, n_col)
    col, row, head = col.reshape(n_row * rays, width), row.reshape(n_col * rays, width), head.reshape(HEAD, width)
    return front_and_factor(row, head, col, *factor_head(head))


def solution(mesh):
    return jax.shard_map(
        shards,
        mesh=mesh,
        in_specs=(P(("row", "col"), None), P(("row", "col")), P(("row", "col"))),
        out_specs=(P("row", "col", None), P("row", None)),
        check_vma=False,
    )
```

```python
import functools

import jax
import jax.numpy as jnp
from jax import lax
from jax.experimental import pallas as pl
from jax.experimental.pallas import tpu as pltpu
from jax.sharding import PartitionSpec as P

PANEL = 256
PANELS = 4
NT = 64
HEAD = PANEL * PANELS
EXTRA = 128
W = 8
B = 128
MESH = pl.DeviceIdType.MESH
HIGHEST = lax.Precision.HIGHEST
F32 = jnp.float32
BF16 = jnp.bfloat16
VMEM = pl.BlockSpec(memory_space=pltpu.VMEM)
ANY = pl.BlockSpec(memory_space=pl.ANY)


def time_rate():
    length = NT / 8.0
    return 1.0 / (2.0 * length * length)


def nn(a, b, precision=None):
    return lax.dot_general(a, b, (((1,), (0,)), ((), ())), precision=precision, preferred_element_type=F32)


def nt(a, b, precision=None):
    return lax.dot_general(a, b, (((1,), (1,)), ((), ())), precision=precision, preferred_element_type=F32)


def tn(a, b, precision=None):
    return lax.dot_general(a, b, (((0,), (0,)), ((), ())), precision=precision, preferred_element_type=F32)


def split(x):
    hi = x.astype(BF16)
    return hi, (x - hi.astype(F32)).astype(BF16)


NX, NZ = 4, 8
QUARTERS = 4


def remote(src, dst, send_sem, recv_sem, device):
    return pltpu.make_async_remote_copy(
        src_ref=src, dst_ref=dst, send_sem=send_sem, recv_sem=recv_sem, device_id=device, device_id_type=MESH
    )


class Feed:
    def __init__(self, n_row, n_col, pay_ref, head_ref, col_ref, row_ref, sems):
        self.n_row, self.n_col = n_row, n_col
        self.pay, self.head, self.col, self.row = pay_ref, head_ref, col_ref, row_ref
        (self.local, self.hsend, self.qrecv, self.hrecv, self.csend, self.crecv, self.xsend, self.xrecv, self.rsend, self.rrecv) = sems
        self.r, self.c = lax.axis_index("row"), lax.axis_index("col")
        self.x, self.z = self.r // NZ, self.r % NZ
        self.ny = n_col // 2
        self.y, self.core = self.c // 2, self.c % 2
        self.rays = pay_ref.shape[0]
        self.part = self.rays // QUARTERS
        self.sends = []

    def at_row(self, x, z):
        return (x * NZ + z, self.c)

    def at_col(self, y, core):
        return (self.r, y * 2 + core)

    def barrier(self):
        sem = pltpu.get_barrier_semaphore()
        for d in range(1, NX):
            pl.semaphore_signal(sem, inc=1, device_id=self.at_row((self.x + d) % NX, self.z), device_id_type=MESH)
        for d in range(1, NZ):
            pl.semaphore_signal(sem, inc=1, device_id=self.at_row(self.x, (self.z + d) % NZ), device_id_type=MESH)
        for d in range(1, self.n_col):
            pl.semaphore_signal(sem, inc=1, device_id=(self.r, (self.c + d) % self.n_col), device_id_type=MESH)
        pl.semaphore_wait(sem, NX + NZ + self.n_col - 3)

    def quarter(self, b, q, device, send):
        where = self.head.at[b * self.n_col + self.c, pl.ds(pl.multiple_of(q * self.part, self.part), self.part)]
        return remote(where, where, self.hsend.at[send], self.qrecv.at[b * QUARTERS + q], device)

    def block(self, b, col, device, send):
        where = self.head.at[b * self.n_col + col]
        return remote(where, where, self.hsend.at[send], self.hrecv.at[b * self.n_col + col], device)

    def send(self, copy, when=None):
        self.sends.append((copy, when))
        if when is None:
            copy.start()
        else:
            pl.when(when)(copy.start)

    def gather_head(self):
        x, y, z, c, core = self.x, self.y, self.z, self.c, self.core
        here = self.at_row(x, z)
        source = [(x == 0) & (z == b) for b in range(2)]
        for b in range(2):
            @pl.when(source[b])
            def _(b=b):
                self.head[b * self.n_col + c] = self.pay[...]

        count = 0
        for b in range(2):
            for q in range(1, QUARTERS):
                self.send(self.quarter(b, q, self.at_row(q, z), count + q - 1), source[b])
        count += QUARTERS - 1
        onward = jnp.where((z >= 1) & (z <= 3), z + 1, (z + NZ - 1) % NZ)
        for b in range(2):
            pl.when(jnp.logical_not(source[b]))(self.quarter(b, x, here, 0).wait_recv)
            self.send(self.quarter(b, x, self.at_row(x, onward), count), (z != 4) & (z != 5))
            self.send(self.quarter(b, x, self.at_row(x, 1 - b), count + 1), z == b)
            for d in range(1, NX):
                to = (x + d) % NX
                self.send(self.quarter(b, x, self.at_row(to, z), count + 1 + d), jnp.logical_not((to == 0) & (z == b)))
            count += 1 + NX
        left, right, across = (y + self.ny - 1) % self.ny, (y + 1) % self.ny, (y + 2) % self.ny
        for b in range(2):
            for d in range(1, NX):
                pl.when(jnp.logical_not(source[b]))(self.quarter(b, (x + d) % NX, here, 0).wait_recv)
            self.send(self.block(b, c, self.at_col(right, core), count))
            self.send(self.block(b, c, self.at_col(left, core), count + 1))
            self.send(self.block(b, c, self.at_col(y, 1 - core), count + 2))
            count += 3
        self.start_columns()
        for b in range(2):
            for near, far, relay in ((left, right, b == 0), (right, left, b == 1)):
                came = near * 2 + core
                self.block(b, came, here, 0).wait_recv()
                if relay:
                    self.send(self.block(b, came, self.at_col(far, core), count))
                    count += 1
                self.send(self.block(b, came, self.at_col(y, 1 - core), count))
                count += 1
        for b in range(2):
            came = across * 2 + core
            self.block(b, came, here, 0).wait_recv()
            self.send(self.block(b, came, self.at_col(y, 1 - core), count))
            count += 1
        self.start_rows()
        for b in range(2):
            for d in range(self.ny):
                self.block(b, ((y + d) % self.ny) * 2 + 1 - core, here, 0).wait_recv()

    def column(self, z, d):
        return remote(
            self.pay, self.col.at[self.x * NZ + z], self.csend.at[d], self.crecv.at[z], self.at_row(self.x, (self.z + d) % NZ)
        )

    def plane(self, x, d):
        where = self.col.at[pl.ds(pl.multiple_of(x * NZ, NZ), NZ)]
        return remote(where, where, self.xsend.at[d], self.xrecv.at[x], self.at_row((self.x + d) % NX, self.z))

    def across_row(self, col, d):
        return remote(self.pay, self.row.at[col], self.rsend.at[d], self.rrecv.at[col], (self.r, (self.c + d) % self.n_col))

    def start_columns(self):
        self.own_col = pltpu.make_async_copy(self.pay, self.col.at[self.r], self.local.at[0])
        self.own_col.start()
        for d in range(1, NZ):
            self.column(self.z, d).start()

    def start_rows(self):
        self.own_row = pltpu.make_async_copy(self.pay, self.row.at[self.c], self.local.at[1])
        self.own_row.start()
        for d in range(1, self.n_col):
            self.across_row(self.c, d).start()

    def start_planes(self):
        self.own_col.wait()
        for d in range(1, NZ):
            self.column((self.z + d) % NZ, d).wait_recv()
        for d in range(1, NX):
            self.plane(self.x, d).start()

    def finish(self):
        self.own_row.wait()
        for d in range(1, self.n_col):
            self.across_row((self.c + d) % self.n_col, d).wait_recv()
        for d in range(1, NX):
            self.plane((self.x + d) % NX, d).wait_recv()
        for copy, when in self.sends:
            if when is None:
                copy.wait_send()
            else:
                pl.when(when)(copy.wait_send)
        for d in range(1, NZ):
            self.column(self.z, d).wait_send()
        for d in range(1, NX):
            self.plane(self.x, d).wait_send()
        for d in range(1, self.n_col):
            self.across_row(self.c, d).wait_send()


def table():
    s = lax.broadcasted_iota(jnp.int32, (EXTRA, 512), 0)
    q = lax.broadcasted_iota(jnp.int32, (EXTRA, 512), 1)
    part = q // NT
    gap = (s - q % NT).astype(F32)
    value = jnp.exp(-gap * gap * time_rate())
    hi = value.astype(BF16).astype(F32)
    mid = (value - hi).astype(BF16).astype(F32)
    low = value - hi - mid
    kernel_part = jnp.where(part == 0, hi, jnp.where(part == 1, mid, jnp.where(part == 2, low, 0.0)))
    chosen = jnp.where(part < 4, kernel_part, jnp.where(gap == 0.0, 1.0, 0.0))
    return jnp.where(s < NT, chosen, 0.0).astype(BF16)


def lookups(extra, tab):
    both = nn(extra, tab).astype(BF16)
    return both[:, :256], both[:, 256:]


def noise_of(extra):
    e = extra[:, NT : NT + 3].astype(F32)
    return (e[:, 0:1] + e[:, 1:2]) + e[:, 2:3]


def factor_block(d_ref):
    lane = lax.broadcasted_iota(jnp.int32, (W, B), 1)
    sub = lax.broadcasted_iota(jnp.int32, (W, B), 0)

    def row(x, i):
        return jnp.broadcast_to(x[i : i + 1, :], (W, B))

    def col(x, i):
        return jnp.broadcast_to(x[:, i : i + 1], (W, B))

    for k in range(B // W):
        lo = W * k
        rows = d_ref[lo : lo + W, :]
        cols = [col(rows, lo + i) for i in range(W)]
        inside = (lane >= lo) & (lane < lo + W)
        rows = jnp.where(inside, jnp.where(lane - lo == sub, 1.0, 0.0), rows)
        done = jnp.zeros((W, B), F32)
        for i in range(W):
            pivot = row(cols[i], i)
            inverse = 1.0 / pivot
            current = row(rows, i)
            done = jnp.where(sub == i, current * lax.rsqrt(pivot), done)
            scaled = current * inverse
            rows = jnp.where(sub == i, scaled, rows - cols[i] * scaled)
            for j in range(i + 1, W):
                entry = row(cols[j], i) * inverse
                cols[j] = jnp.where(sub == i, entry, cols[j] - cols[i] * entry)
        d_ref[lo : lo + W, :] = done
        spread = [row(rows, i) for i in range(W)]
        for m in range(k + 1, B // W):
            other = d_ref[W * m : W * m + W, :]
            total = jnp.where(inside, 0.0, other)
            for i in range(W):
                total = total - col(other, lo + i) * spread[i]
            d_ref[W * m : W * m + W, :] = total


def factor_head(head_ref, uhi_ref, ulo_ref, whi_ref, wlo_ref, s_ref, w_ref, d_ref, midway):
    n = HEAD // B
    feat = head_ref[:, : head_ref.shape[1] - EXTRA]
    extra = head_ref[:, head_ref.shape[1] - EXTRA :]
    value, hot = lookups(extra, table())
    noise = noise_of(extra)
    for i in range(n):
        rs = slice(B * i, B * i + B)
        rr = lax.broadcasted_iota(jnp.int32, (B, HEAD - B * i), 0)
        cc = lax.broadcasted_iota(jnp.int32, (B, HEAD - B * i), 1)
        s_ref[rs, B * i :] = nt(feat[rs], feat[B * i :]) * nt(value[rs], hot[B * i :]) + jnp.where(rr == cc, noise[rs], 0.0)

    r = lax.broadcasted_iota(jnp.int32, (B, B), 0)
    c = lax.broadcasted_iota(jnp.int32, (B, B), 1)

    def tail(j):
        def go():
            lo = B * (j + 1)
            if lo >= HEAD:
                return
            solved = nn(w_ref[j], s_ref[lo - B : lo, lo:], HIGHEST)
            s_ref[lo - B : lo, lo:] = solved
            uhi_ref[lo - B : lo, lo:], ulo_ref[lo - B : lo, lo:] = split(solved)
            for i in range(j + 1, n):
                at = B * (i - j - 1)
                s_ref[B * i : B * i + B, B * i :] -= tn(solved[:, at : at + B], solved[:, at:], HIGHEST)

        return go

    def step(j, carry):
        at = pl.multiple_of(j * B, B)
        d_ref[...] = s_ref[pl.ds(at, B), pl.ds(at, B)]
        factor_block(d_ref)
        w_ref[j] = jnp.where(r >= c, d_ref[...], 0.0)
        lax.switch(j, [tail(i) for i in range(n)])
        return carry

    lax.fori_loop(0, 2, step, 0)
    midway()
    lax.fori_loop(2, n, step, 0)
    for p in range(PANELS):
        a, b = w_ref[2 * p], w_ref[2 * p + 1]
        low = -nn(b, tn(s_ref[PANEL * p : PANEL * p + B, PANEL * p + B : PANEL * p + PANEL], a, HIGHEST), HIGHEST)
        for x, rs, cs in ((a, slice(0, B), slice(0, B)), (low, slice(B, PANEL), slice(0, B)), (b, slice(B, PANEL), slice(B, PANEL))):
            whi_ref[p, rs, cs], wlo_ref[p, rs, cs] = split(x)
        whi_ref[p, :B, B:] = jnp.zeros((B, B), BF16)
        wlo_ref[p, :B, B:] = jnp.zeros((B, B), BF16)


def head_kernel(n_row, n_col, pay_ref, col_ref, row_ref, out_head_ref, uhi_ref, ulo_ref, whi_ref, wlo_ref, blocks_ref, head_ref, s_ref, w_ref, d_ref, *sems):
    feed = Feed(n_row, n_col, pay_ref, blocks_ref, col_ref, row_ref, sems)
    feed.barrier()
    feed.gather_head()
    rays = feed.rays
    for i in range(HEAD // rays):
        head_ref[i * rays : i * rays + rays, :] = blocks_ref[i]
    out = pltpu.make_async_copy(head_ref, out_head_ref, feed.local.at[2])
    out.start()
    factor_head(head_ref, uhi_ref, ulo_ref, whi_ref, wlo_ref, s_ref, w_ref, d_ref, feed.start_planes)
    feed.finish()
    out.wait()


def gather_and_factor(payload, n_row, n_col):
    rays, width = payload.shape
    dma = pltpu.SemaphoreType.DMA
    return pl.pallas_call(
        functools.partial(head_kernel, n_row, n_col),
        out_shape=(
            jax.ShapeDtypeStruct((n_row, rays, width), BF16),
            jax.ShapeDtypeStruct((n_col, rays, width), BF16),
            jax.ShapeDtypeStruct((HEAD, width), BF16),
            jax.ShapeDtypeStruct((HEAD, HEAD), BF16),
            jax.ShapeDtypeStruct((HEAD, HEAD), BF16),
            jax.ShapeDtypeStruct((PANELS, PANEL, PANEL), BF16),
            jax.ShapeDtypeStruct((PANELS, PANEL, PANEL), BF16),
        ),
        in_specs=[VMEM],
        out_specs=(ANY, ANY, ANY, VMEM, VMEM, VMEM, VMEM),
        scratch_shapes=[
            pltpu.VMEM((HEAD // rays, rays, width), BF16),
            pltpu.VMEM((HEAD, width), BF16),
            pltpu.VMEM((HEAD, HEAD), F32),
            pltpu.VMEM((HEAD // B, B, B), F32),
            pltpu.VMEM((B, B), F32),
            dma((3,)), dma((32,)), dma((2 * QUARTERS,)), dma((2 * n_col,)), dma((NZ,)), dma((NZ,)), dma((NX,)), dma((NX,)), dma((n_col,)), dma((n_col,)),
        ],
        compiler_params=pltpu.CompilerParams(collective_id=0, has_side_effects=True, vmem_limit_bytes=40 << 20),
        name="gather_and_factor",
    )(payload)


def front_kernel(row_ref, head_ref, col_ref, uhi_ref, ulo_ref, whi_ref, wlo_ref, front_ref, factor_ref, tab_ref, hhot_ref, rval_ref, rhi_ref, rlo_ref, hi_ref, lo_ref):
    step = pl.program_id(0)
    r, c = lax.axis_index("row"), lax.axis_index("col")
    f = head_ref.shape[1] - EXTRA
    rows = row_ref.shape[0]
    tile = col_ref.shape[0]
    rays = rows // lax.axis_size("col")

    def solve(ref, value, noise, hi_out, lo_out):
        feat = ref[:, :f]
        n = ref.shape[0]
        for p in range(PANELS):
            ps = slice(PANEL * p, PANEL * p + PANEL)
            x = nt(feat, head_ref[ps, :f]) * nt(value, hhot_ref[ps])
            if noise is not None:
                rr = r * n + lax.broadcasted_iota(jnp.int32, (n, PANEL), 0)
                cc = PANEL * p + lax.broadcasted_iota(jnp.int32, (n, PANEL), 1)
                x = x + jnp.where(rr == cc, noise, 0.0)
            if p > 0:
                k = PANEL * p
                x = x - (nn(hi_out[:, :k], uhi_ref[:k, ps]) + (nn(hi_out[:, :k], ulo_ref[:k, ps]) + nn(lo_out[:, :k], uhi_ref[:k, ps])))
            xh, xl = split(x)
            s = nt(xh, whi_ref[p]) + (nt(xh, wlo_ref[p]) + nt(xl, whi_ref[p]))
            hi_out[:, ps], lo_out[:, ps] = split(s)
            if noise is not None:
                factor_ref[:, ps] = jnp.where(rr >= cc, s, 0.0)

    @pl.when(step == 0)
    def _():
        tab_ref[...] = table()
        hhot_ref[...] = lookups(head_ref[:, f:], tab_ref[...])[1]
        rval_ref[...] = lookups(row_ref[:, f:], tab_ref[...])[0]
        solve(row_ref, rval_ref[...], noise_of(row_ref[:, f:]), rhi_ref, rlo_ref)

    value, hot = lookups(col_ref[:, f:], tab_ref[...])
    solve(col_ref, value, None, hi_ref, lo_ref)
    full = nt(row_ref[:, :f], col_ref[:, :f]) * nt(rval_ref[...], hot)
    ri = lax.broadcasted_iota(jnp.int32, (rows, tile), 0)
    li = step * tile + lax.broadcasted_iota(jnp.int32, (rows, tile), 1)
    col_local = li - r * rays
    full = full + jnp.where(ri - c * rays == col_local, jnp.where((col_local >= 0) & (col_local < rays), noise_of(row_ref[:, f:]), 0.0), 0.0)
    full = full - (nt(rhi_ref[...], hi_ref[...]) + (nt(rhi_ref[...], lo_ref[...]) + nt(rlo_ref[...], hi_ref[...])))
    first = jnp.where(r >= HEAD // rows, HEAD // (rows // rays * rays) * rays, tile * pl.num_programs(0))
    front_ref[:, 0, :] = jnp.where(li >= first, full, 0.0)


def front_and_factor(row, head, col, uhi, ulo, whi, wlo):
    rows, width = row.shape
    cols = col.shape[0]
    tile = 512
    whole = lambda a: pl.BlockSpec(a.shape, lambda i: (0,) * a.ndim)
    return pl.pallas_call(
        front_kernel,
        grid=(cols // tile,),
        out_shape=(jax.ShapeDtypeStruct((rows, 1, cols), F32), jax.ShapeDtypeStruct((rows, HEAD), F32)),
        in_specs=[whole(row), whole(head), pl.BlockSpec((tile, width), lambda i: (i, 0)), whole(uhi), whole(ulo), whole(whi), whole(wlo)],
        out_specs=(pl.BlockSpec((rows, 1, tile), lambda i: (0, 0, i)), pl.BlockSpec((rows, HEAD), lambda i: (0, 0))),
        scratch_shapes=[
            pltpu.VMEM((EXTRA, 512), BF16),
            pltpu.VMEM((HEAD, 256), BF16),
            pltpu.VMEM((rows, 256), BF16),
            pltpu.VMEM((rows, HEAD), BF16),
            pltpu.VMEM((rows, HEAD), BF16),
            pltpu.VMEM((tile, HEAD), BF16),
            pltpu.VMEM((tile, HEAD), BF16),
        ],
        compiler_params=pltpu.CompilerParams(vmem_limit_bytes=56 << 20),
        name="front_and_factor",
    )(row, head, col, uhi, ulo, whi, wlo)


def shards(features, slot_of_ray, noise):
    n_row, n_col = lax.axis_size("row"), lax.axis_size("col")
    rays = noise.shape[0]
    lanes = jnp.arange(EXTRA, dtype=jnp.int32)[None, :]
    hi = lax.reduce_precision(noise, 8, 7)
    mid = lax.reduce_precision(noise - hi, 8, 7)
    low = noise - hi - mid
    extra = jnp.where(lanes == slot_of_ray[:, None], 1.0, 0.0)
    for i, part in enumerate((hi, mid, low)):
        extra = jnp.where(lanes == NT + i, part[:, None], extra)
    payload = jnp.concatenate([features, extra.astype(BF16)], axis=1)
    width = payload.shape[1]
    col, row, head, *factors = gather_and_factor(payload, n_row, n_col)
    return front_and_factor(row.reshape(n_col * rays, width), head, col.reshape(n_row * rays, width), *factors)


def solution(mesh):
    return jax.shard_map(
        shards,
        mesh=mesh,
        in_specs=(P(("row", "col"), None), P(("row", "col")), P(("row", "col"))),
        out_specs=(P("row", "col", None), P("row", None)),
        check_vma=False,
    )
```

```python
import functools

import jax
import jax.numpy as jnp
from jax import lax
from jax.experimental import pallas as pl
from jax.experimental.pallas import tpu as pltpu
from jax.sharding import PartitionSpec as P

PANEL = 256
PANELS = 4
NT = 64
HEAD = PANEL * PANELS
EXTRA = 128
W = 8
B = 128
MESH = pl.DeviceIdType.MESH
HIGHEST = lax.Precision.HIGHEST
F32 = jnp.float32
BF16 = jnp.bfloat16
VMEM = pl.BlockSpec(memory_space=pltpu.VMEM)
ANY = pl.BlockSpec(memory_space=pl.ANY)


def time_rate():
    length = NT / 8.0
    return 1.0 / (2.0 * length * length)


def nn(a, b, precision=None):
    return lax.dot_general(a, b, (((1,), (0,)), ((), ())), precision=precision, preferred_element_type=F32)


def nt(a, b, precision=None):
    return lax.dot_general(a, b, (((1,), (1,)), ((), ())), precision=precision, preferred_element_type=F32)


def tn(a, b, precision=None):
    return lax.dot_general(a, b, (((0,), (0,)), ((), ())), precision=precision, preferred_element_type=F32)


def split(x):
    hi = x.astype(BF16)
    return hi, (x - hi.astype(F32)).astype(BF16)


NX, NZ = 4, 8
PANEL_PAIRS = [(p, q) for q in range(PANELS) for p in range(q)]


def remote(src, dst, send_sem, recv_sem, device):
    return pltpu.make_async_remote_copy(
        src_ref=src, dst_ref=dst, send_sem=send_sem, recv_sem=recv_sem, device_id=device, device_id_type=MESH
    )


class Feed:
    def __init__(self, n_row, n_col, pay_ref, head_ref, col_ref, row_ref, sems):
        self.n_row, self.n_col = n_row, n_col
        self.pay, self.head, self.col, self.row = pay_ref, head_ref, col_ref, row_ref
        (self.local, self.hsend, self.hrecv, self.csend, self.crecv, self.xsend, self.xrecv, self.rsend, self.rrecv) = sems
        self.r, self.c = lax.axis_index("row"), lax.axis_index("col")
        self.x, self.z = self.r // NZ, self.r % NZ
        self.ny = n_col // 2
        self.y, self.core = self.c // 2, self.c % 2
        self.rays = pay_ref.shape[0]
        self.part = self.rays // NX
        self.sends = []

    def at_row(self, x, z):
        return (x * NZ + z, self.c)

    def at_col(self, y, core):
        return (self.r, y * 2 + core)

    def barrier(self):
        sem = pltpu.get_barrier_semaphore()
        for d in range(1, NX):
            pl.semaphore_signal(sem, inc=1, device_id=self.at_row((self.x + d) % NX, self.z), device_id_type=MESH)
        for d in range(1, NZ):
            pl.semaphore_signal(sem, inc=1, device_id=self.at_row(self.x, (self.z + d) % NZ), device_id_type=MESH)
        for d in range(1, self.n_col):
            pl.semaphore_signal(sem, inc=1, device_id=(self.r, (self.c + d) % self.n_col), device_id_type=MESH)
        pl.semaphore_wait(sem, NX + NZ + self.n_col - 3)

    def rows_of(self, q):
        return pl.ds(pl.multiple_of(q * self.part, self.part), self.part)

    def send(self, src, dst, recv, device, when=None):
        copy = remote(src, dst, self.hsend.at[len(self.sends)], self.hrecv.at[recv], device)
        self.sends.append((copy, when))
        if when is None:
            copy.start()
        else:
            pl.when(when)(copy.start)

    def arrived(self, dst, recv, when=None):
        copy = remote(dst, dst, self.hsend.at[0], self.hrecv.at[recv], (self.r, self.c))
        if when is None:
            copy.wait_recv()
        else:
            pl.when(when)(copy.wait_recv)

    def gather_head(self):
        x, y, z, core, ny = self.x, self.y, self.z, self.core, self.ny
        head = self.head
        x_first, y_first, y_then, x_then, other = 2, 2 + NX, 2 + NX + ny, 2 + NX + 2 * ny, 2 + 2 * NX + 2 * ny
        own = [head.at[b, core, y, self.rows_of(x)] for b in range(2)]
        for b in range(2):
            here = (x == 0) & (z == b)

            @pl.when(here)
            def _(b=b):
                head[b, core, y, 0 : self.part] = self.pay[0 : self.part]

            for q in range(1, NX):
                part = pl.ds(q * self.part, self.part)
                self.send(self.pay.at[part], head.at[b, core, y, part], b, self.at_row(q, z), here)
        for b in range(2):
            self.arrived(own[b], b, jnp.logical_not((x == 0) | (z != b)))
            for d in range(1, NZ):
                self.send(own[b], own[b], b, self.at_row(x, (z + d) % NZ), z == b)
        for b in range(2):
            self.arrived(own[b], b, z != b)
        for d in range(1, NX):
            self.send(own[0], own[0], x_first + x, self.at_row((x + d) % NX, z))
        for d in range(1, ny):
            self.send(own[1], own[1], y_first + y, self.at_col((y + d) % ny, core))
        self.start_columns()
        for d in range(1, NX):
            self.arrived(own[0], x_first + (x + d) % NX)
        block = head.at[0, core, y]
        for d in range(1, ny):
            self.send(block, block, y_then + y, self.at_col((y + d) % ny, core))
        for d in range(1, ny):
            self.arrived(own[1], y_first + (y + d) % ny)
        strip = head.at[1, core, :, self.rows_of(x)]
        for d in range(1, NX):
            self.send(strip, strip, x_then + x, self.at_row((x + d) % NX, z))
        self.start_rows()
        for d in range(1, ny):
            self.arrived(block, y_then + (y + d) % ny)
        self.send(head.at[0, core], head.at[0, core], other, self.at_col(y, 1 - core))
        for d in range(1, NX):
            self.arrived(strip, x_then + (x + d) % NX)
        self.send(head.at[1, core], head.at[1, core], other + 1, self.at_col(y, 1 - core))
        for b in range(2):
            self.arrived(head.at[b, core], other + b)

    def column(self, z, d):
        return remote(
            self.pay, self.col.at[self.x * NZ + z], self.csend.at[d], self.crecv.at[z], self.at_row(self.x, (self.z + d) % NZ)
        )

    def plane(self, i):
        left, right = (self.x + NX - 1) % NX, (self.x + 1) % NX
        start, count = ((self.x * NZ, NZ), (self.x * NZ, NZ), (left * NZ, NZ // 2), (right * NZ + NZ // 2, NZ // 2))[i]
        where = self.col.at[pl.ds(start, count)]
        return remote(where, where, self.xsend.at[i], self.xrecv.at[i], self.at_row(left if i % 2 else right, self.z))

    def across_row(self, col, d):
        return remote(self.pay, self.row.at[col], self.rsend.at[d], self.rrecv.at[col], (self.r, (self.c + d) % self.n_col))

    def start_columns(self):
        self.own_col = pltpu.make_async_copy(self.pay, self.col.at[self.r], self.local.at[0])
        self.own_col.start()
        for d in range(1, NZ):
            self.column(self.z, d).start()

    def start_rows(self):
        self.own_row = pltpu.make_async_copy(self.pay, self.row.at[self.c], self.local.at[1])
        self.own_row.start()
        for d in range(1, self.n_col):
            self.across_row(self.c, d).start()

    def start_planes(self):
        self.own_col.wait()
        for d in range(1, NZ):
            self.column((self.z + d) % NZ, d).wait_recv()
        self.plane(0).start()
        self.plane(1).start()

    def relay_planes(self):
        for i in (0, 1):
            self.plane(i).wait_recv()
            self.plane(i + 2).start()

    def finish(self):
        self.own_row.wait()
        for d in range(1, self.n_col):
            self.across_row((self.c + d) % self.n_col, d).wait_recv()
        for i in (2, 3):
            self.plane(i).wait_recv()
        for copy, when in self.sends:
            if when is None:
                copy.wait_send()
            else:
                pl.when(when)(copy.wait_send)
        for d in range(1, NZ):
            self.column(self.z, d).wait_send()
        for i in range(4):
            self.plane(i).wait_send()
        for d in range(1, self.n_col):
            self.across_row(self.c, d).wait_send()


def table():
    s = lax.broadcasted_iota(jnp.int32, (EXTRA, 512), 0)
    q = lax.broadcasted_iota(jnp.int32, (EXTRA, 512), 1)
    part = q // NT
    gap = (s - q % NT).astype(F32)
    value = jnp.exp(-gap * gap * time_rate())
    hi = value.astype(BF16).astype(F32)
    mid = (value - hi).astype(BF16).astype(F32)
    low = value - hi - mid
    kernel_part = jnp.where(part == 0, hi, jnp.where(part == 1, mid, jnp.where(part == 2, low, 0.0)))
    chosen = jnp.where(part < 4, kernel_part, jnp.where(gap == 0.0, 1.0, 0.0))
    return jnp.where(s < NT, chosen, 0.0).astype(BF16)


def lookups(extra, tab):
    both = nn(extra, tab).astype(BF16)
    return both[:, :256], both[:, 256:]


def noise_of(extra):
    e = extra[:, NT : NT + 3].astype(F32)
    return (e[:, 0:1] + e[:, 1:2]) + e[:, 2:3]


def factor_block(d_ref, chores):
    lane = lax.broadcasted_iota(jnp.int32, (W, B), 1)
    sub = lax.broadcasted_iota(jnp.int32, (W, B), 0)

    def row(x, i):
        return jnp.broadcast_to(x[i : i + 1, :], (W, B))

    def col(x, i):
        return jnp.broadcast_to(x[:, i : i + 1], (W, B))

    steps = B // W
    for k in range(steps):
        lo = W * k
        rows = d_ref[lo : lo + W, :]
        work = [col(rows, lo + i) for i in range(W)]
        inside = (lane >= lo) & (lane < lo + W)
        work.append(jnp.where(inside, jnp.where(lane - lo == sub, 1.0, 0.0), rows))
        done = jnp.zeros((W, B), F32)
        for i in range(0, W, 2):
            first, second = work[i], work[i + 1]
            a, b, d = row(first, i), row(second, i), row(second, i + 1)
            det = a * d - b * b
            inverse = 1.0 / det
            for j in range(i + 2, W + 1):
                x0, x1 = row(work[j], i), row(work[j], i + 1)
                u0 = d * x0 - b * x1
                u1 = a * x1 - b * x0
                if j == W:
                    done = jnp.where(sub == i, x0 * lax.rsqrt(a), done)
                    done = jnp.where(sub == i + 1, u1 * (lax.rsqrt(a) * lax.rsqrt(det)), done)
                pivots = jnp.where(sub == i, u0, u1) * inverse
                others = work[j] - (first * u0 + second * u1) * inverse
                work[j] = jnp.where((sub == i) | (sub == i + 1), pivots, others)
        d_ref[lo : lo + W, :] = done
        spread = [row(work[W], i) for i in range(W)]
        for m in range(k + 1, steps):
            other = d_ref[W * m : W * m + W, :]
            terms = [col(other, lo + i) * spread[i] for i in range(W)]
            while len(terms) > 1:
                terms = [sum(terms[i : i + 2]) for i in range(0, len(terms), 2)]
            d_ref[W * m : W * m + W, :] = jnp.where(inside, 0.0, other) - terms[0]
        for chore in chores[len(chores) * k // steps : len(chores) * (k + 1) // steps]:
            chore()


def factor_head(head_ref, uhi_ref, ulo_ref, whi_ref, wlo_ref, s_ref, w_ref, d_ref, hooks):
    n = HEAD // B
    f = head_ref.shape[1] - EXTRA
    extra = head_ref[:, f:]
    value, hot = lookups(extra, table())
    noise = noise_of(extra)

    def build(i):
        rs = slice(B * i, B * i + B)
        rr = lax.broadcasted_iota(jnp.int32, (B, HEAD - B * i), 0)
        cc = lax.broadcasted_iota(jnp.int32, (B, HEAD - B * i), 1)
        s_ref[rs, B * i :] = nt(head_ref[rs, :f], head_ref[B * i :, :f]) * nt(value[rs], hot[B * i :]) + jnp.where(rr == cc, noise[rs], 0.0)

    def put_u(p, rs, q, cs, x):
        if p < q:
            uhi_ref[PANEL_PAIRS.index((p, q)), rs, cs], ulo_ref[PANEL_PAIRS.index((p, q)), rs, cs] = split(x)

    def put_w(p, rs, cs, x):
        whi_ref[p, rs, cs], wlo_ref[p, rs, cs] = split(x)

    def half(i):
        return slice(B * (i % 2), B * (i % 2) + B)

    r = lax.broadcasted_iota(jnp.int32, (B, B), 0)
    c = lax.broadcasted_iota(jnp.int32, (B, B), 1)
    blk = lambda i: slice(B * i, B * i + B)

    def solve(j, i):
        solved = nn(w_ref[j], s_ref[blk(j), blk(i)], HIGHEST)
        s_ref[blk(j), blk(i)] = solved
        put_u(j // 2, half(j), i // 2, half(i), solved)

    def update(j, i, m):
        s_ref[blk(i), blk(m)] -= tn(s_ref[blk(j), blk(i)], s_ref[blk(j), blk(m)], HIGHEST)

    def finish_pair(p):
        a, b = w_ref[2 * p], w_ref[2 * p + 1]
        low = -nn(b, tn(s_ref[blk(2 * p), blk(2 * p + 1)], a, HIGHEST), HIGHEST)
        put_w(p, slice(0, B), slice(0, B), a)
        put_w(p, slice(B, PANEL), slice(0, B), low)
        put_w(p, slice(B, PANEL), slice(B, PANEL), b)
        put_w(p, slice(0, B), slice(B, PANEL), jnp.zeros((B, B), F32))

    build(0)
    chores = [functools.partial(build, i) for i in range(1, n)]
    for j in range(n):
        if j in hooks:
            hooks[j]()
        d_ref[...] = s_ref[blk(j), blk(j)]
        factor_block(d_ref, chores)
        w_ref[j] = jnp.where(r >= c, d_ref[...], 0.0)
        if j + 1 < n:
            solve(j, j + 1)
            update(j, j + 1, j + 1)
        chores = [functools.partial(solve, j, i) for i in range(j + 2, n)]
        chores += [functools.partial(update, j, i, m) for i in range(j + 1, n) for m in range(i, n) if m > j + 1]
        if j % 2:
            chores.append(functools.partial(finish_pair, j // 2))
    for chore in chores:
        chore()


def head_kernel(n_row, n_col, pay_ref, col_ref, row_ref, out_head_ref, uhi_ref, ulo_ref, whi_ref, wlo_ref, blocks_ref, head_ref, s_ref, w_ref, d_ref, *sems):
    feed = Feed(n_row, n_col, pay_ref, blocks_ref, col_ref, row_ref, sems)
    feed.barrier()
    feed.gather_head()
    rays = feed.rays
    for i in range(HEAD // rays):
        head_ref[i * rays : i * rays + rays, :] = blocks_ref[i // n_col, i % 2, i % n_col // 2]
    out = pltpu.make_async_copy(head_ref, out_head_ref, feed.local.at[2])
    out.start()
    factor_head(head_ref, uhi_ref, ulo_ref, whi_ref, wlo_ref, s_ref, w_ref, d_ref, {2: feed.start_planes, 5: feed.relay_planes})
    feed.finish()
    out.wait()


def gather_and_factor(payload, n_row, n_col):
    rays, width = payload.shape
    dma = pltpu.SemaphoreType.DMA
    return pl.pallas_call(
        functools.partial(head_kernel, n_row, n_col),
        out_shape=(
            jax.ShapeDtypeStruct((n_row, rays, width), BF16),
            jax.ShapeDtypeStruct((n_col, rays, width), BF16),
            jax.ShapeDtypeStruct((HEAD, width), BF16),
            jax.ShapeDtypeStruct((len(PANEL_PAIRS), PANEL, PANEL), BF16),
            jax.ShapeDtypeStruct((len(PANEL_PAIRS), PANEL, PANEL), BF16),
            jax.ShapeDtypeStruct((PANELS, PANEL, PANEL), BF16),
            jax.ShapeDtypeStruct((PANELS, PANEL, PANEL), BF16),
        ),
        in_specs=[VMEM],
        out_specs=(ANY, ANY, ANY, VMEM, VMEM, VMEM, VMEM),
        scratch_shapes=[
            pltpu.VMEM((2, 2, n_col // 2, rays, width), BF16),
            pltpu.VMEM((HEAD, width), BF16),
            pltpu.VMEM((HEAD, HEAD), F32),
            pltpu.VMEM((HEAD // B, B, B), F32),
            pltpu.VMEM((B, B), F32),
            dma((3,)), dma((48,)), dma((32,)), dma((NZ,)), dma((NZ,)), dma((4,)), dma((4,)), dma((n_col,)), dma((n_col,)),
        ],
        compiler_params=pltpu.CompilerParams(collective_id=0, has_side_effects=True, vmem_limit_bytes=40 << 20),
        name="gather_and_factor",
    )(payload)


def front_kernel(row_ref, head_ref, col_ref, uhi_ref, ulo_ref, whi_ref, wlo_ref, front_ref, factor_ref, tab_ref, hhot_ref, rval_ref, rhi_ref, rlo_ref, hi_ref, lo_ref):
    step = pl.program_id(0)
    r, c = lax.axis_index("row"), lax.axis_index("col")
    f = head_ref.shape[1] - EXTRA
    rows = row_ref.shape[0]
    tile = col_ref.shape[0]
    rays = rows // lax.axis_size("col")

    def solve(ref, value, noise, hi_out, lo_out):
        feat = ref[:, :f]
        n = ref.shape[0]
        for p in range(PANELS):
            ps = slice(PANEL * p, PANEL * p + PANEL)
            x = nt(feat, head_ref[ps, :f]) * nt(value, hhot_ref[ps])
            if noise is not None:
                rr = r * n + lax.broadcasted_iota(jnp.int32, (n, PANEL), 0)
                cc = PANEL * p + lax.broadcasted_iota(jnp.int32, (n, PANEL), 1)
                x = x + jnp.where(rr == cc, noise, 0.0)
            for q in range(p):
                qs = slice(PANEL * q, PANEL * q + PANEL)
                at = PANEL_PAIRS.index((q, p))
                x = x - (nn(hi_out[:, qs], uhi_ref[at]) + (nn(hi_out[:, qs], ulo_ref[at]) + nn(lo_out[:, qs], uhi_ref[at])))
            xh, xl = split(x)
            s = nt(xh, whi_ref[p]) + (nt(xh, wlo_ref[p]) + nt(xl, whi_ref[p]))
            hi_out[:, ps], lo_out[:, ps] = split(s)
            if noise is not None:
                factor_ref[:, ps] = jnp.where(rr >= cc, s, 0.0)

    @pl.when(step == 0)
    def _():
        tab_ref[...] = table()
        hhot_ref[...] = lookups(head_ref[:, f:], tab_ref[...])[1]
        rval_ref[...] = lookups(row_ref[:, f:], tab_ref[...])[0]
        solve(row_ref, rval_ref[...], noise_of(row_ref[:, f:]), rhi_ref, rlo_ref)

    value, hot = lookups(col_ref[:, f:], tab_ref[...])
    solve(col_ref, value, None, hi_ref, lo_ref)
    full = nt(row_ref[:, :f], col_ref[:, :f]) * nt(rval_ref[...], hot)
    ri = lax.broadcasted_iota(jnp.int32, (rows, tile), 0)
    li = step * tile + lax.broadcasted_iota(jnp.int32, (rows, tile), 1)
    col_local = li - r * rays
    full = full + jnp.where(ri - c * rays == col_local, jnp.where((col_local >= 0) & (col_local < rays), noise_of(row_ref[:, f:]), 0.0), 0.0)
    full = full - (nt(rhi_ref[...], hi_ref[...]) + (nt(rhi_ref[...], lo_ref[...]) + nt(rlo_ref[...], hi_ref[...])))
    first = jnp.where(r >= HEAD // rows, HEAD // (rows // rays * rays) * rays, tile * pl.num_programs(0))
    front_ref[:, 0, :] = jnp.where(li >= first, full, 0.0)


def front_and_factor(row, head, col, uhi, ulo, whi, wlo):
    rows, width = row.shape
    cols = col.shape[0]
    tile = 512
    whole = lambda a: pl.BlockSpec(a.shape, lambda i: (0,) * a.ndim)
    return pl.pallas_call(
        front_kernel,
        grid=(cols // tile,),
        out_shape=(jax.ShapeDtypeStruct((rows, 1, cols), F32), jax.ShapeDtypeStruct((rows, HEAD), F32)),
        in_specs=[whole(row), whole(head), pl.BlockSpec((tile, width), lambda i: (i, 0)), whole(uhi), whole(ulo), whole(whi), whole(wlo)],
        out_specs=(pl.BlockSpec((rows, 1, tile), lambda i: (0, 0, i)), pl.BlockSpec((rows, HEAD), lambda i: (0, 0))),
        scratch_shapes=[
            pltpu.VMEM((EXTRA, 512), BF16),
            pltpu.VMEM((HEAD, 256), BF16),
            pltpu.VMEM((rows, 256), BF16),
            pltpu.VMEM((rows, HEAD), BF16),
            pltpu.VMEM((rows, HEAD), BF16),
            pltpu.VMEM((tile, HEAD), BF16),
            pltpu.VMEM((tile, HEAD), BF16),
        ],
        compiler_params=pltpu.CompilerParams(vmem_limit_bytes=56 << 20),
        name="front_and_factor",
    )(row, head, col, uhi, ulo, whi, wlo)


def shards(features, slot_of_ray, noise):
    n_row, n_col = lax.axis_size("row"), lax.axis_size("col")
    rays = noise.shape[0]
    lanes = jnp.arange(EXTRA, dtype=jnp.int32)[None, :]
    hi = lax.reduce_precision(noise, 8, 7)
    mid = lax.reduce_precision(noise - hi, 8, 7)
    low = noise - hi - mid
    extra = jnp.where(lanes == slot_of_ray[:, None], 1.0, 0.0)
    for i, part in enumerate((hi, mid, low)):
        extra = jnp.where(lanes == NT + i, part[:, None], extra)
    payload = jnp.concatenate([features, extra.astype(BF16)], axis=1)
    width = payload.shape[1]
    col, row, head, *factors = gather_and_factor(payload, n_row, n_col)
    return front_and_factor(row.reshape(n_col * rays, width), head, col.reshape(n_row * rays, width), *factors)


def solution(mesh):
    return jax.shard_map(
        shards,
        mesh=mesh,
        in_specs=(P(("row", "col"), None), P(("row", "col")), P(("row", "col"))),
        out_specs=(P("row", "col", None), P("row", None)),
        check_vma=False,
    )
```

```python
import functools

import jax
import jax.numpy as jnp
from jax import lax
from jax.experimental import pallas as pl
from jax.experimental.pallas import tpu as pltpu
from jax.sharding import PartitionSpec as P

PANEL = 256
PANELS = 4
NT = 64
HEAD = PANEL * PANELS
EXTRA = 128
W = 8
B = 128
MESH = pl.DeviceIdType.MESH
HIGHEST = lax.Precision.HIGHEST
F32 = jnp.float32
BF16 = jnp.bfloat16
VMEM = pl.BlockSpec(memory_space=pltpu.VMEM)
ANY = pl.BlockSpec(memory_space=pl.ANY)


def time_rate():
    length = NT / 8.0
    return 1.0 / (2.0 * length * length)


def nn(a, b, precision=None):
    return lax.dot_general(a, b, (((1,), (0,)), ((), ())), precision=precision, preferred_element_type=F32)


def nt(a, b, precision=None):
    return lax.dot_general(a, b, (((1,), (1,)), ((), ())), precision=precision, preferred_element_type=F32)


def tn(a, b, precision=None):
    return lax.dot_general(a, b, (((0,), (0,)), ((), ())), precision=precision, preferred_element_type=F32)


def split(x):
    hi = x.astype(BF16)
    return hi, (x - hi.astype(F32)).astype(BF16)


NX, NZ = 4, 8
TRIANGLE = PANELS * (PANELS + 1) // 2


def remote(src, dst, send_sem, recv_sem, device):
    return pltpu.make_async_remote_copy(
        src_ref=src, dst_ref=dst, send_sem=send_sem, recv_sem=recv_sem, device_id=device, device_id_type=MESH
    )


class Feed:
    def __init__(self, n_row, n_col, pay_ref, head_ref, col_ref, row_ref, sems):
        self.n_row, self.n_col = n_row, n_col
        self.pay, self.head, self.col, self.row = pay_ref, head_ref, col_ref, row_ref
        (self.local, self.hsend, self.hrecv, self.csend, self.crecv, self.xsend, self.xrecv, self.rsend, self.rrecv) = sems
        self.r, self.c = lax.axis_index("row"), lax.axis_index("col")
        self.x, self.z = self.r // NZ, self.r % NZ
        self.ny = n_col // 2
        self.y, self.core = self.c // 2, self.c % 2
        self.rays = pay_ref.shape[0]
        self.part = self.rays // NX
        self.sends = []

    def at_row(self, x, z):
        return (x * NZ + z, self.c)

    def at_col(self, y, core):
        return (self.r, y * 2 + core)

    def barrier(self):
        sem = pltpu.get_barrier_semaphore()
        for d in range(1, NX):
            pl.semaphore_signal(sem, inc=1, device_id=self.at_row((self.x + d) % NX, self.z), device_id_type=MESH)
        for d in range(1, NZ):
            pl.semaphore_signal(sem, inc=1, device_id=self.at_row(self.x, (self.z + d) % NZ), device_id_type=MESH)
        for d in range(1, self.n_col):
            pl.semaphore_signal(sem, inc=1, device_id=(self.r, (self.c + d) % self.n_col), device_id_type=MESH)
        pl.semaphore_wait(sem, NX + NZ + self.n_col - 3)

    def rows_of(self, q):
        return pl.ds(pl.multiple_of(q * self.part, self.part), self.part)

    def send(self, src, dst, recv, device, when=None):
        copy = remote(src, dst, self.hsend.at[len(self.sends)], self.hrecv.at[recv], device)
        self.sends.append((copy, when))
        if when is None:
            copy.start()
        else:
            pl.when(when)(copy.start)

    def arrived(self, dst, recv, when=None):
        copy = remote(dst, dst, self.hsend.at[0], self.hrecv.at[recv], (self.r, self.c))
        if when is None:
            copy.wait_recv()
        else:
            pl.when(when)(copy.wait_recv)

    def gather_head(self):
        x, y, z, core, ny = self.x, self.y, self.z, self.core, self.ny
        head = self.head
        x_first, y_first, y_then, x_then, other = 2, 2 + NX, 2 + NX + ny, 2 + NX + 2 * ny, 2 + 2 * NX + 2 * ny
        own = [head.at[b, core, y, self.rows_of(x)] for b in range(2)]
        for b in range(2):
            here = (x == 0) & (z == b)

            @pl.when(here)
            def _(b=b):
                head[b, core, y, 0 : self.part] = self.pay[0 : self.part]

            for q in range(1, NX):
                part = pl.ds(q * self.part, self.part)
                self.send(self.pay.at[part], head.at[b, core, y, part], b, self.at_row(q, z), here)
        for b in range(2):
            self.arrived(own[b], b, jnp.logical_not((x == 0) | (z != b)))
            for d in range(1, NZ):
                self.send(own[b], own[b], b, self.at_row(x, (z + d) % NZ), z == b)
        for b in range(2):
            self.arrived(own[b], b, z != b)
        for d in range(1, NX):
            self.send(own[0], own[0], x_first + x, self.at_row((x + d) % NX, z))
        for d in range(1, ny):
            self.send(own[1], own[1], y_first + y, self.at_col((y + d) % ny, core))
        self.start_columns()
        for d in range(1, NX):
            self.arrived(own[0], x_first + (x + d) % NX)
        block = head.at[0, core, y]
        for d in range(1, ny):
            self.send(block, block, y_then + y, self.at_col((y + d) % ny, core))
        for d in range(1, ny):
            self.arrived(own[1], y_first + (y + d) % ny)
        strip = head.at[1, core, :, self.rows_of(x)]
        for d in range(1, NX):
            self.send(strip, strip, x_then + x, self.at_row((x + d) % NX, z))
        self.start_rows()
        for d in range(1, ny):
            self.arrived(block, y_then + (y + d) % ny)
        self.send(head.at[0, core], head.at[0, core], other, self.at_col(y, 1 - core))
        for d in range(1, NX):
            self.arrived(strip, x_then + (x + d) % NX)
        self.send(head.at[1, core], head.at[1, core], other + 1, self.at_col(y, 1 - core))
        for b in range(2):
            self.arrived(head.at[b, core], other + b)

    def column(self, z, d):
        return remote(
            self.pay, self.col.at[self.x * NZ + z], self.csend.at[d], self.crecv.at[z], self.at_row(self.x, (self.z + d) % NZ)
        )

    def plane(self, i):
        left, right = (self.x + NX - 1) % NX, (self.x + 1) % NX
        start, count = ((self.x * NZ, NZ), (self.x * NZ, NZ), (left * NZ, NZ // 2), (right * NZ + NZ // 2, NZ // 2))[i]
        where = self.col.at[pl.ds(start, count)]
        return remote(where, where, self.xsend.at[i], self.xrecv.at[i], self.at_row(left if i % 2 else right, self.z))

    def across_row(self, col, d):
        return remote(self.pay, self.row.at[col], self.rsend.at[d], self.rrecv.at[col], (self.r, (self.c + d) % self.n_col))

    def start_columns(self):
        self.own_col = pltpu.make_async_copy(self.pay, self.col.at[self.r], self.local.at[0])
        self.own_col.start()
        for d in range(1, NZ):
            self.column(self.z, d).start()

    def start_rows(self):
        self.own_row = pltpu.make_async_copy(self.pay, self.row.at[self.c], self.local.at[1])
        self.own_row.start()
        for d in range(1, self.n_col):
            self.across_row(self.c, d).start()

    def start_planes(self):
        self.own_col.wait()
        for d in range(1, NZ):
            self.column((self.z + d) % NZ, d).wait_recv()
        self.plane(0).start()
        self.plane(1).start()

    def relay_planes(self):
        for i in (0, 1):
            self.plane(i).wait_recv()
            self.plane(i + 2).start()

    def finish(self):
        self.own_row.wait()
        for d in range(1, self.n_col):
            self.across_row((self.c + d) % self.n_col, d).wait_recv()
        for i in (2, 3):
            self.plane(i).wait_recv()
        for copy, when in self.sends:
            if when is None:
                copy.wait_send()
            else:
                pl.when(when)(copy.wait_send)
        for d in range(1, NZ):
            self.column(self.z, d).wait_send()
        for i in range(4):
            self.plane(i).wait_send()
        for d in range(1, self.n_col):
            self.across_row(self.c, d).wait_send()


def table():
    s = lax.broadcasted_iota(jnp.int32, (EXTRA, 512), 0)
    q = lax.broadcasted_iota(jnp.int32, (EXTRA, 512), 1)
    part = q // NT
    gap = (s - q % NT).astype(F32)
    value = jnp.exp(-gap * gap * time_rate())
    hi = value.astype(BF16).astype(F32)
    mid = (value - hi).astype(BF16).astype(F32)
    low = value - hi - mid
    kernel_part = jnp.where(part == 0, hi, jnp.where(part == 1, mid, jnp.where(part == 2, low, 0.0)))
    chosen = jnp.where(part < 4, kernel_part, jnp.where(gap == 0.0, 1.0, 0.0))
    return jnp.where(s < NT, chosen, 0.0).astype(BF16)


def lookups(extra, tab):
    both = nn(extra, tab).astype(BF16)
    return both[:, :256], both[:, 256:]


def noise_of(extra):
    e = extra[:, NT : NT + 3].astype(F32)
    return (e[:, 0:1] + e[:, 1:2]) + e[:, 2:3]


def factor_block(d_ref, chores):
    lane = lax.broadcasted_iota(jnp.int32, (W, B), 1)
    sub = lax.broadcasted_iota(jnp.int32, (W, B), 0)

    def row(x, i):
        return jnp.broadcast_to(x[i : i + 1, :], (W, B))

    def col(x, i):
        return jnp.broadcast_to(x[:, i : i + 1], (W, B))

    steps = B // W
    for k in range(steps):
        lo = W * k
        rows = d_ref[lo : lo + W, :]
        work = [col(rows, lo + i) for i in range(W)]
        inside = (lane >= lo) & (lane < lo + W)
        work.append(jnp.where(inside, jnp.where(lane - lo == sub, 1.0, 0.0), rows))
        done = jnp.zeros((W, B), F32)
        for i in range(0, W, 2):
            first, second = work[i], work[i + 1]
            a, b, d = row(first, i), row(second, i), row(second, i + 1)
            det = a * d - b * b
            inverse = 1.0 / det
            for j in range(i + 2, W + 1):
                x0, x1 = row(work[j], i), row(work[j], i + 1)
                u0 = d * x0 - b * x1
                u1 = a * x1 - b * x0
                if j == W:
                    done = jnp.where(sub == i, x0 * lax.rsqrt(a), done)
                    done = jnp.where(sub == i + 1, u1 * (lax.rsqrt(a) * lax.rsqrt(det)), done)
                pivots = jnp.where(sub == i, u0, u1) * inverse
                others = work[j] - (first * u0 + second * u1) * inverse
                work[j] = jnp.where((sub == i) | (sub == i + 1), pivots, others)
        d_ref[lo : lo + W, :] = done
        spread = [row(work[W], i) for i in range(W)]
        for m in range(k + 1, steps):
            other = d_ref[W * m : W * m + W, :]
            terms = [col(other, lo + i) * spread[i] for i in range(W)]
            while len(terms) > 1:
                terms = [sum(terms[i : i + 2]) for i in range(0, len(terms), 2)]
            d_ref[W * m : W * m + W, :] = jnp.where(inside, 0.0, other) - terms[0]
        for chore in chores[len(chores) * k // steps : len(chores) * (k + 1) // steps]:
            chore()


def factor_head(head_ref, thi_ref, tlo_ref, s_ref, w_ref, t_ref, d_ref, hooks):
    n = HEAD // B
    f = head_ref.shape[1] - EXTRA
    extra = head_ref[:, f:]
    value, hot = lookups(extra, table())
    noise = noise_of(extra)

    def build(i):
        rs = slice(B * i, B * i + B)
        rr = lax.broadcasted_iota(jnp.int32, (B, HEAD - B * i), 0)
        cc = lax.broadcasted_iota(jnp.int32, (B, HEAD - B * i), 1)
        s_ref[rs, B * i :] = nt(head_ref[rs, :f], head_ref[B * i :, :f]) * nt(value[rs], hot[B * i :]) + jnp.where(rr == cc, noise[rs], 0.0)

    r = lax.broadcasted_iota(jnp.int32, (B, B), 0)
    c = lax.broadcasted_iota(jnp.int32, (B, B), 1)
    blk = lambda i: slice(B * i, B * i + B)

    def solve(j, i):
        solved = nn(w_ref[j], s_ref[blk(j), blk(i)], HIGHEST)
        s_ref[blk(j), blk(i)] = solved

    def update(j, i, m):
        s_ref[blk(i), blk(m)] -= tn(s_ref[blk(j), blk(i)], s_ref[blk(j), blk(m)], HIGHEST)

    pan = lambda p: slice(PANEL * p, PANEL * p + PANEL)
    spot = lambda p, q: p * (p + 1) // 2 + q

    def put(p, q, value):
        t_ref[spot(p, q)] = value
        thi_ref[spot(p, q)], tlo_ref[spot(p, q)] = split(value)

    def inverse_diagonal(p):
        a, b = w_ref[2 * p], w_ref[2 * p + 1]
        upper = -nt(tn(a, s_ref[blk(2 * p), blk(2 * p + 1)], HIGHEST), b, HIGHEST)
        zero = jnp.zeros((B, B), F32)
        put(p, p, jnp.concatenate([jnp.concatenate([a.T, upper], axis=1), jnp.concatenate([zero, b.T], axis=1)], axis=0))

    def inverse_sum(p, q):
        total = nn(t_ref[spot(q, q)], s_ref[pan(q), pan(p)], HIGHEST)
        for k in range(q + 1, p):
            total = total + nn(t_ref[spot(k, q)], s_ref[pan(k), pan(p)], HIGHEST)
        t_ref[spot(p, q)] = total

    def inverse_row(p, q):
        put(p, q, -nn(t_ref[spot(p, q)], t_ref[spot(p, p)], HIGHEST))

    build(0)
    chores = [functools.partial(build, i) for i in range(1, n)]
    for j in range(n):
        if j in hooks:
            hooks[j]()
        d_ref[...] = s_ref[blk(j), blk(j)]
        factor_block(d_ref, chores)
        w_ref[j] = jnp.where(r >= c, d_ref[...], 0.0)
        if j + 1 < n:
            solve(j, j + 1)
            update(j, j + 1, j + 1)
        chores = [functools.partial(solve, j, i) for i in range(j + 2, n)]
        chores += [functools.partial(update, j, i, m) for i in range(j + 1, n) for m in range(i, n) if m > j + 1]
        if j % 2:
            chores.append(functools.partial(inverse_diagonal, j // 2))
            chores += [functools.partial(inverse_row, j // 2, q) for q in range(j // 2)]
        elif j:
            chores += [functools.partial(inverse_sum, j // 2, q) for q in range(j // 2)]
    for chore in chores:
        chore()


def head_kernel(n_row, n_col, pay_ref, col_ref, row_ref, out_head_ref, thi_ref, tlo_ref, blocks_ref, head_ref, s_ref, w_ref, t_ref, d_ref, *sems):
    feed = Feed(n_row, n_col, pay_ref, blocks_ref, col_ref, row_ref, sems)
    feed.barrier()
    feed.gather_head()
    rays = feed.rays
    for i in range(HEAD // rays):
        head_ref[i * rays : i * rays + rays, :] = blocks_ref[i // n_col, i % 2, i % n_col // 2]
    out = pltpu.make_async_copy(head_ref, out_head_ref, feed.local.at[2])
    out.start()
    factor_head(head_ref, thi_ref, tlo_ref, s_ref, w_ref, t_ref, d_ref, {2: feed.start_planes, 5: feed.relay_planes})
    feed.finish()
    out.wait()


def gather_and_factor(payload, n_row, n_col):
    rays, width = payload.shape
    dma = pltpu.SemaphoreType.DMA
    return pl.pallas_call(
        functools.partial(head_kernel, n_row, n_col),
        out_shape=(
            jax.ShapeDtypeStruct((n_row, rays, width), BF16),
            jax.ShapeDtypeStruct((n_col, rays, width), BF16),
            jax.ShapeDtypeStruct((HEAD, width), BF16),
            jax.ShapeDtypeStruct((TRIANGLE, PANEL, PANEL), BF16),
            jax.ShapeDtypeStruct((TRIANGLE, PANEL, PANEL), BF16),
        ),
        in_specs=[VMEM],
        out_specs=(ANY, ANY, ANY, VMEM, VMEM),
        scratch_shapes=[
            pltpu.VMEM((2, 2, n_col // 2, rays, width), BF16),
            pltpu.VMEM((HEAD, width), BF16),
            pltpu.VMEM((HEAD, HEAD), F32),
            pltpu.VMEM((HEAD // B, B, B), F32),
            pltpu.VMEM((TRIANGLE, PANEL, PANEL), F32),
            pltpu.VMEM((B, B), F32),
            dma((3,)), dma((48,)), dma((32,)), dma((NZ,)), dma((NZ,)), dma((4,)), dma((4,)), dma((n_col,)), dma((n_col,)),
        ],
        compiler_params=pltpu.CompilerParams(collective_id=0, has_side_effects=True, vmem_limit_bytes=40 << 20),
        name="gather_and_factor",
    )(payload)


def front_kernel(row_ref, head_ref, col_ref, thi_ref, tlo_ref, front_ref, factor_ref, tab_ref, hhot_ref, rval_ref, rhi_ref, rlo_ref, hi_ref, lo_ref, mhi_ref, mlo_ref):
    step = pl.program_id(0)
    r, c = lax.axis_index("row"), lax.axis_index("col")
    f = head_ref.shape[1] - EXTRA
    rows = row_ref.shape[0]
    tile = col_ref.shape[0]
    rays = rows // lax.axis_size("col")

    def solve(ref, value, noise, hi_out, lo_out):
        feat = ref[:, :f]
        n = ref.shape[0]
        for p in range(PANELS):
            ps = slice(PANEL * p, PANEL * p + PANEL)
            x = nt(feat, head_ref[ps, :f]) * nt(value, hhot_ref[ps])
            if noise is not None:
                rr = r * n + lax.broadcasted_iota(jnp.int32, (n, PANEL), 0)
                cc = PANEL * p + lax.broadcasted_iota(jnp.int32, (n, PANEL), 1)
                x = x + jnp.where(rr == cc, noise, 0.0)
            mhi_ref[:, ps], mlo_ref[:, ps] = split(x)
        for p in range(PANELS):
            ps = slice(PANEL * p, PANEL * p + PANEL)
            k = PANEL * (p + 1)
            at = p * (p + 1) // 2
            th, tl = thi_ref[at : at + p + 1].reshape(k, PANEL), tlo_ref[at : at + p + 1].reshape(k, PANEL)
            s = nn(mhi_ref[:, :k], th) + (nn(mhi_ref[:, :k], tl) + nn(mlo_ref[:, :k], th))
            hi_out[:, ps], lo_out[:, ps] = split(s)
            if noise is not None:
                rr = r * n + lax.broadcasted_iota(jnp.int32, (n, PANEL), 0)
                cc = PANEL * p + lax.broadcasted_iota(jnp.int32, (n, PANEL), 1)
                factor_ref[:, ps] = jnp.where(rr >= cc, s, 0.0)

    @pl.when(step == 0)
    def _():
        tab_ref[...] = table()
        hhot_ref[...] = lookups(head_ref[:, f:], tab_ref[...])[1]
        rval_ref[...] = lookups(row_ref[:, f:], tab_ref[...])[0]
        solve(row_ref, rval_ref[...], noise_of(row_ref[:, f:]), rhi_ref, rlo_ref)

    value, hot = lookups(col_ref[:, f:], tab_ref[...])
    solve(col_ref, value, None, hi_ref, lo_ref)
    full = nt(row_ref[:, :f], col_ref[:, :f]) * nt(rval_ref[...], hot)
    ri = lax.broadcasted_iota(jnp.int32, (rows, tile), 0)
    li = step * tile + lax.broadcasted_iota(jnp.int32, (rows, tile), 1)
    col_local = li - r * rays
    full = full + jnp.where(ri - c * rays == col_local, jnp.where((col_local >= 0) & (col_local < rays), noise_of(row_ref[:, f:]), 0.0), 0.0)
    full = full - (nt(rhi_ref[...], hi_ref[...]) + (nt(rhi_ref[...], lo_ref[...]) + nt(rlo_ref[...], hi_ref[...])))
    first = jnp.where(r >= HEAD // rows, HEAD // (rows // rays * rays) * rays, tile * pl.num_programs(0))
    front_ref[:, 0, :] = jnp.where(li >= first, full, 0.0)


def front_and_factor(row, head, col, thi, tlo):
    rows, width = row.shape
    cols = col.shape[0]
    tile = 512
    whole = lambda a: pl.BlockSpec(a.shape, lambda i: (0,) * a.ndim)
    return pl.pallas_call(
        front_kernel,
        grid=(cols // tile,),
        out_shape=(jax.ShapeDtypeStruct((rows, 1, cols), F32), jax.ShapeDtypeStruct((rows, HEAD), F32)),
        in_specs=[whole(row), whole(head), pl.BlockSpec((tile, width), lambda i: (i, 0)), whole(thi), whole(tlo)],
        out_specs=(pl.BlockSpec((rows, 1, tile), lambda i: (0, 0, i)), pl.BlockSpec((rows, HEAD), lambda i: (0, 0))),
        scratch_shapes=[
            pltpu.VMEM((EXTRA, 512), BF16),
            pltpu.VMEM((HEAD, 256), BF16),
            pltpu.VMEM((rows, 256), BF16),
            pltpu.VMEM((rows, HEAD), BF16),
            pltpu.VMEM((rows, HEAD), BF16),
            pltpu.VMEM((tile, HEAD), BF16),
            pltpu.VMEM((tile, HEAD), BF16),
            pltpu.VMEM((max(tile, rows), HEAD), BF16),
            pltpu.VMEM((max(tile, rows), HEAD), BF16),
        ],
        compiler_params=pltpu.CompilerParams(vmem_limit_bytes=63 << 20),
        name="front_and_factor",
    )(row, head, col, thi, tlo)


def shards(features, slot_of_ray, noise):
    n_row, n_col = lax.axis_size("row"), lax.axis_size("col")
    rays = noise.shape[0]
    lanes = jnp.arange(EXTRA, dtype=jnp.int32)[None, :]
    hi = lax.reduce_precision(noise, 8, 7)
    mid = lax.reduce_precision(noise - hi, 8, 7)
    low = noise - hi - mid
    extra = jnp.where(lanes == slot_of_ray[:, None], 1.0, 0.0)
    for i, part in enumerate((hi, mid, low)):
        extra = jnp.where(lanes == NT + i, part[:, None], extra)
    payload = jnp.concatenate([features, extra.astype(BF16)], axis=1)
    width = payload.shape[1]
    col, row, head, *factors = gather_and_factor(payload, n_row, n_col)
    return front_and_factor(row.reshape(n_col * rays, width), head, col.reshape(n_row * rays, width), *factors)


def solution(mesh):
    return jax.shard_map(
        shards,
        mesh=mesh,
        in_specs=(P(("row", "col"), None), P(("row", "col")), P(("row", "col"))),
        out_specs=(P("row", "col", None), P("row", None)),
        check_vma=False,
    )
```

```python
import functools

import jax
import jax.numpy as jnp
from jax import lax
from jax.experimental import pallas as pl
from jax.experimental.pallas import tpu as pltpu
from jax.sharding import PartitionSpec as P

PANEL = 256
PANELS = 4
NT = 64
HEAD = PANEL * PANELS
EXTRA = 128
W = 8
B = 128
MESH = pl.DeviceIdType.MESH
HIGHEST = lax.Precision.HIGHEST
F32 = jnp.float32
BF16 = jnp.bfloat16
VMEM = pl.BlockSpec(memory_space=pltpu.VMEM)
ANY = pl.BlockSpec(memory_space=pl.ANY)


def time_rate():
    length = NT / 8.0
    return 1.0 / (2.0 * length * length)


def nn(a, b, precision=None):
    return lax.dot_general(a, b, (((1,), (0,)), ((), ())), precision=precision, preferred_element_type=F32)


def nt(a, b, precision=None):
    return lax.dot_general(a, b, (((1,), (1,)), ((), ())), precision=precision, preferred_element_type=F32)


def tn(a, b, precision=None):
    return lax.dot_general(a, b, (((0,), (0,)), ((), ())), precision=precision, preferred_element_type=F32)


def split(x):
    hi = x.astype(BF16)
    return hi, (x - hi.astype(F32)).astype(BF16)


NX, NZ = 4, 8
TRIANGLE = PANELS * (PANELS + 1) // 2


def remote(src, dst, send_sem, recv_sem, device):
    return pltpu.make_async_remote_copy(
        src_ref=src, dst_ref=dst, send_sem=send_sem, recv_sem=recv_sem, device_id=device, device_id_type=MESH
    )


class Feed:
    def __init__(self, n_row, n_col, pay_ref, head_ref, col_ref, row_ref, sems):
        self.n_row, self.n_col = n_row, n_col
        self.pay, self.head, self.col, self.row = pay_ref, head_ref, col_ref, row_ref
        (self.local, self.hsend, self.hrecv, self.csend, self.crecv, self.xsend, self.xrecv, self.rsend, self.rrecv) = sems
        self.r, self.c = lax.axis_index("row"), lax.axis_index("col")
        self.x, self.z = self.r // NZ, self.r % NZ
        self.ny = n_col // 2
        self.y, self.core = self.c // 2, self.c % 2
        self.rays = pay_ref.shape[0]
        self.part = self.rays // NX
        self.sends = []

    def at_row(self, x, z):
        return (x * NZ + z, self.c)

    def at_col(self, y, core):
        return (self.r, y * 2 + core)

    def barrier(self):
        sem = pltpu.get_barrier_semaphore()
        for d in range(1, NX):
            pl.semaphore_signal(sem, inc=1, device_id=self.at_row((self.x + d) % NX, self.z), device_id_type=MESH)
        for d in range(1, NZ):
            pl.semaphore_signal(sem, inc=1, device_id=self.at_row(self.x, (self.z + d) % NZ), device_id_type=MESH)
        for d in range(1, self.n_col):
            pl.semaphore_signal(sem, inc=1, device_id=(self.r, (self.c + d) % self.n_col), device_id_type=MESH)
        pl.semaphore_wait(sem, NX + NZ + self.n_col - 3)

    def rows_of(self, q):
        return pl.ds(pl.multiple_of(q * self.part, self.part), self.part)

    def send(self, src, dst, recv, device, when=None):
        copy = remote(src, dst, self.hsend.at[len(self.sends)], self.hrecv.at[recv], device)
        self.sends.append((copy, when))
        if when is None:
            copy.start()
        else:
            pl.when(when)(copy.start)

    def arrived(self, dst, recv, when=None):
        copy = remote(dst, dst, self.hsend.at[0], self.hrecv.at[recv], (self.r, self.c))
        if when is None:
            copy.wait_recv()
        else:
            pl.when(when)(copy.wait_recv)

    def gather_head(self):
        x, y, z, core, ny = self.x, self.y, self.z, self.core, self.ny
        head = self.head
        x_first, y_first, y_then, x_then, other = 2, 2 + NX, 2 + NX + ny, 2 + NX + 2 * ny, 2 + 2 * NX + 2 * ny
        own = [head.at[b, core, y, self.rows_of(x)] for b in range(2)]
        for b in range(2):
            here = (x == 0) & (z == b)

            @pl.when(here)
            def _(b=b):
                head[b, core, y, 0 : self.part] = self.pay[0 : self.part]

            for q in range(1, NX):
                part = pl.ds(q * self.part, self.part)
                self.send(self.pay.at[part], head.at[b, core, y, part], b, self.at_row(q, z), here)
        for b in range(2):
            self.arrived(own[b], b, jnp.logical_not((x == 0) | (z != b)))
            for d in range(1, NZ):
                self.send(own[b], own[b], b, self.at_row(x, (z + d) % NZ), z == b)
        for b in range(2):
            self.arrived(own[b], b, z != b)
        for d in range(1, NX):
            self.send(own[0], own[0], x_first + x, self.at_row((x + d) % NX, z))
        for d in range(1, ny):
            self.send(own[1], own[1], y_first + y, self.at_col((y + d) % ny, core))
        self.start_columns()
        for d in range(1, NX):
            self.arrived(own[0], x_first + (x + d) % NX)
        block = head.at[0, core, y]
        for d in range(1, ny):
            self.send(block, block, y_then + y, self.at_col((y + d) % ny, core))
        for d in range(1, ny):
            self.arrived(own[1], y_first + (y + d) % ny)
        strip = head.at[1, core, :, self.rows_of(x)]
        for d in range(1, NX):
            self.send(strip, strip, x_then + x, self.at_row((x + d) % NX, z))
        self.start_rows()
        for d in range(1, ny):
            self.arrived(block, y_then + (y + d) % ny)
        self.send(head.at[0, core], head.at[0, core], other, self.at_col(y, 1 - core))
        for d in range(1, NX):
            self.arrived(strip, x_then + (x + d) % NX)
        self.send(head.at[1, core], head.at[1, core], other + 1, self.at_col(y, 1 - core))
        for b in range(2):
            self.arrived(head.at[b, core], other + b)

    def column(self, z, d):
        return remote(
            self.pay, self.col.at[self.x * NZ + z], self.csend.at[d], self.crecv.at[z], self.at_row(self.x, (self.z + d) % NZ)
        )

    def plane(self, i):
        left, right = (self.x + NX - 1) % NX, (self.x + 1) % NX
        start, count = ((self.x * NZ, NZ), (self.x * NZ, NZ), (left * NZ, NZ // 2), (right * NZ + NZ // 2, NZ // 2))[i]
        where = self.col.at[pl.ds(start, count)]
        return remote(where, where, self.xsend.at[i], self.xrecv.at[i], self.at_row(left if i % 2 else right, self.z))

    def across_row(self, col, d):
        return remote(self.pay, self.row.at[col], self.rsend.at[d], self.rrecv.at[col], (self.r, (self.c + d) % self.n_col))

    def start_columns(self):
        self.own_col = pltpu.make_async_copy(self.pay, self.col.at[self.r], self.local.at[0])
        self.own_col.start()
        for d in range(1, NZ):
            self.column(self.z, d).start()

    def start_rows(self):
        self.own_row = pltpu.make_async_copy(self.pay, self.row.at[self.c], self.local.at[1])
        self.own_row.start()
        for d in range(1, self.n_col):
            self.across_row(self.c, d).start()

    def start_planes(self):
        self.own_col.wait()
        for d in range(1, NZ):
            self.column((self.z + d) % NZ, d).wait_recv()
        self.plane(0).start()
        self.plane(1).start()

    def relay_planes(self):
        for i in (0, 1):
            self.plane(i).wait_recv()
            self.plane(i + 2).start()

    def finish(self):
        self.own_row.wait()
        for d in range(1, self.n_col):
            self.across_row((self.c + d) % self.n_col, d).wait_recv()
        for i in (2, 3):
            self.plane(i).wait_recv()
        for copy, when in self.sends:
            if when is None:
                copy.wait_send()
            else:
                pl.when(when)(copy.wait_send)
        for d in range(1, NZ):
            self.column(self.z, d).wait_send()
        for i in range(4):
            self.plane(i).wait_send()
        for d in range(1, self.n_col):
            self.across_row(self.c, d).wait_send()


def table():
    s = lax.broadcasted_iota(jnp.int32, (EXTRA, 512), 0)
    q = lax.broadcasted_iota(jnp.int32, (EXTRA, 512), 1)
    part = q // NT
    gap = (s - q % NT).astype(F32)
    value = jnp.exp(-gap * gap * time_rate())
    hi = value.astype(BF16).astype(F32)
    mid = (value - hi).astype(BF16).astype(F32)
    low = value - hi - mid
    kernel_part = jnp.where(part == 0, hi, jnp.where(part == 1, mid, jnp.where(part == 2, low, 0.0)))
    chosen = jnp.where(part < 4, kernel_part, jnp.where(gap == 0.0, 1.0, 0.0))
    return jnp.where(s < NT, chosen, 0.0).astype(BF16)


def lookups(extra, tab):
    both = nn(extra, tab).astype(BF16)
    return both[:, :256], both[:, 256:]


def noise_of(extra):
    e = extra[:, NT : NT + 3].astype(F32)
    return (e[:, 0:1] + e[:, 1:2]) + e[:, 2:3]


def factor_block(d_ref, chores):
    lane = lax.broadcasted_iota(jnp.int32, (W, B), 1)
    sub = lax.broadcasted_iota(jnp.int32, (W, B), 0)

    def row(x, i):
        return jnp.broadcast_to(x[i : i + 1, :], (W, B))

    def col(x, i):
        return jnp.broadcast_to(x[:, i : i + 1], (W, B))

    steps = B // W
    for k in range(steps):
        lo = W * k
        rows = d_ref[lo : lo + W, :]
        work = [col(rows, lo + i) for i in range(W)]
        inside = (lane >= lo) & (lane < lo + W)
        work.append(jnp.where(inside, jnp.where(lane - lo == sub, 1.0, 0.0), rows))
        done = jnp.zeros((W, B), F32)
        for i in range(0, W, 2):
            first, second = work[i], work[i + 1]
            a, b, d = row(first, i), row(second, i), row(second, i + 1)
            det = a * d - b * b
            inverse = 1.0 / det
            for j in range(i + 2, W + 1):
                x0, x1 = row(work[j], i), row(work[j], i + 1)
                u0 = d * x0 - b * x1
                u1 = a * x1 - b * x0
                if j == W:
                    done = jnp.where(sub == i, x0 * lax.rsqrt(a), done)
                    done = jnp.where(sub == i + 1, u1 * (lax.rsqrt(a) * lax.rsqrt(det)), done)
                pivots = jnp.where(sub == i, u0, u1) * inverse
                others = work[j] - (first * u0 + second * u1) * inverse
                work[j] = jnp.where((sub == i) | (sub == i + 1), pivots, others)
        d_ref[lo : lo + W, :] = done
        spread = [row(work[W], i) for i in range(W)]
        for m in range(k + 1, steps):
            other = d_ref[W * m : W * m + W, :]
            terms = [col(other, lo + i) * spread[i] for i in range(W)]
            while len(terms) > 1:
                terms = [sum(terms[i : i + 2]) for i in range(0, len(terms), 2)]
            d_ref[W * m : W * m + W, :] = jnp.where(inside, 0.0, other) - terms[0]
        for chore in chores[len(chores) * k // steps : len(chores) * (k + 1) // steps]:
            chore()


def factor_head(head_ref, thi_ref, tlo_ref, s_ref, w_ref, t_ref, d_ref, hooks):
    n = HEAD // B
    f = head_ref.shape[1] - EXTRA
    extra = head_ref[:, f:]
    value, hot = lookups(extra, table())
    noise = noise_of(extra)

    def build(i):
        rs = slice(B * i, B * i + B)
        rr = lax.broadcasted_iota(jnp.int32, (B, HEAD - B * i), 0)
        cc = lax.broadcasted_iota(jnp.int32, (B, HEAD - B * i), 1)
        s_ref[rs, B * i :] = nt(head_ref[rs, :f], head_ref[B * i :, :f]) * nt(value[rs], hot[B * i :]) + jnp.where(rr == cc, noise[rs], 0.0)

    r = lax.broadcasted_iota(jnp.int32, (B, B), 0)
    c = lax.broadcasted_iota(jnp.int32, (B, B), 1)
    blk = lambda i: slice(B * i, B * i + B)

    def solve(j, i):
        solved = nn(w_ref[j], s_ref[blk(j), blk(i)], HIGHEST)
        s_ref[blk(j), blk(i)] = solved

    def update(j, i, m):
        s_ref[blk(i), blk(m)] -= tn(s_ref[blk(j), blk(i)], s_ref[blk(j), blk(m)], HIGHEST)

    pan = lambda p: slice(PANEL * p, PANEL * p + PANEL)
    spot = lambda p, q: p * (p + 1) // 2 + q

    def put(p, q, value):
        t_ref[spot(p, q)] = value
        thi_ref[spot(p, q)], tlo_ref[spot(p, q)] = split(value)

    def inverse_diagonal(p):
        a, b = w_ref[2 * p], w_ref[2 * p + 1]
        upper = -nt(tn(a, s_ref[blk(2 * p), blk(2 * p + 1)], HIGHEST), b, HIGHEST)
        zero = jnp.zeros((B, B), F32)
        put(p, p, jnp.concatenate([jnp.concatenate([a.T, upper], axis=1), jnp.concatenate([zero, b.T], axis=1)], axis=0))

    def inverse_sum(p, q):
        total = nn(t_ref[spot(q, q)], s_ref[pan(q), pan(p)], HIGHEST)
        for k in range(q + 1, p):
            total = total + nn(t_ref[spot(k, q)], s_ref[pan(k), pan(p)], HIGHEST)
        t_ref[spot(p, q)] = total

    def inverse_row(p, q):
        put(p, q, -nn(t_ref[spot(p, q)], t_ref[spot(p, p)], HIGHEST))

    build(0)
    chores = [functools.partial(build, i) for i in range(1, n)]
    for j in range(n):
        if j in hooks:
            hooks[j]()
        d_ref[...] = s_ref[blk(j), blk(j)]
        factor_block(d_ref, chores)
        w_ref[j] = jnp.where(r >= c, d_ref[...], 0.0)
        if j + 1 < n:
            solve(j, j + 1)
            update(j, j + 1, j + 1)
        chores = [functools.partial(solve, j, i) for i in range(j + 2, n)]
        chores += [functools.partial(update, j, i, m) for i in range(j + 1, n) for m in range(i, n) if m > j + 1]
        if j % 2:
            chores.append(functools.partial(inverse_diagonal, j // 2))
            chores += [functools.partial(inverse_row, j // 2, q) for q in range(j // 2)]
        elif j:
            chores += [functools.partial(inverse_sum, j // 2, q) for q in range(j // 2)]
    for chore in chores:
        chore()


def head_kernel(n_row, n_col, pay_ref, col_ref, row_ref, out_head_ref, thi_ref, tlo_ref, blocks_ref, head_ref, s_ref, w_ref, t_ref, d_ref, *sems):
    feed = Feed(n_row, n_col, pay_ref, blocks_ref, col_ref, row_ref, sems)
    feed.barrier()
    feed.gather_head()
    rays = feed.rays
    for i in range(HEAD // rays):
        head_ref[i * rays : i * rays + rays, :] = blocks_ref[i // n_col, i % 2, i % n_col // 2]
    out = pltpu.make_async_copy(head_ref, out_head_ref, feed.local.at[2])
    out.start()
    factor_head(head_ref, thi_ref, tlo_ref, s_ref, w_ref, t_ref, d_ref, {1: feed.start_planes, 6: feed.relay_planes})
    feed.finish()
    out.wait()


def gather_and_factor(payload, n_row, n_col):
    rays, width = payload.shape
    dma = pltpu.SemaphoreType.DMA
    return pl.pallas_call(
        functools.partial(head_kernel, n_row, n_col),
        out_shape=(
            jax.ShapeDtypeStruct((n_row, rays, width), BF16),
            jax.ShapeDtypeStruct((n_col, rays, width), BF16),
            jax.ShapeDtypeStruct((HEAD, width), BF16),
            jax.ShapeDtypeStruct((TRIANGLE, PANEL, PANEL), BF16),
            jax.ShapeDtypeStruct((TRIANGLE, PANEL, PANEL), BF16),
        ),
        in_specs=[VMEM],
        out_specs=(ANY, ANY, ANY, VMEM, VMEM),
        scratch_shapes=[
            pltpu.VMEM((2, 2, n_col // 2, rays, width), BF16),
            pltpu.VMEM((HEAD, width), BF16),
            pltpu.VMEM((HEAD, HEAD), F32),
            pltpu.VMEM((HEAD // B, B, B), F32),
            pltpu.VMEM((TRIANGLE, PANEL, PANEL), F32),
            pltpu.VMEM((B, B), F32),
            dma((3,)), dma((48,)), dma((32,)), dma((NZ,)), dma((NZ,)), dma((4,)), dma((4,)), dma((n_col,)), dma((n_col,)),
        ],
        compiler_params=pltpu.CompilerParams(collective_id=0, has_side_effects=True, vmem_limit_bytes=40 << 20),
        name="gather_and_factor",
    )(payload)


def front_kernel(row_ref, head_ref, col_ref, thi_ref, tlo_ref, front_ref, factor_ref, tab_ref, hhot_ref, rval_ref, rhi_ref, rlo_ref, hi_ref, lo_ref, mhi_ref, mlo_ref):
    step = pl.program_id(0)
    r, c = lax.axis_index("row"), lax.axis_index("col")
    f = head_ref.shape[1] - EXTRA
    rows = row_ref.shape[0]
    tile = col_ref.shape[0]
    rays = rows // lax.axis_size("col")

    def solve(ref, value, noise, hi_out, lo_out):
        feat = ref[:, :f]
        n = ref.shape[0]
        for p in range(PANELS):
            ps = slice(PANEL * p, PANEL * p + PANEL)
            x = nt(feat, head_ref[ps, :f]) * nt(value, hhot_ref[ps])
            if noise is not None:
                rr = r * n + lax.broadcasted_iota(jnp.int32, (n, PANEL), 0)
                cc = PANEL * p + lax.broadcasted_iota(jnp.int32, (n, PANEL), 1)
                x = x + jnp.where(rr == cc, noise, 0.0)
            mhi_ref[:, ps], mlo_ref[:, ps] = split(x)
        for p in range(PANELS):
            ps = slice(PANEL * p, PANEL * p + PANEL)
            k = PANEL * (p + 1)
            at = p * (p + 1) // 2
            th, tl = thi_ref[at : at + p + 1].reshape(k, PANEL), tlo_ref[at : at + p + 1].reshape(k, PANEL)
            s = nn(mhi_ref[:, :k], th) + (nn(mhi_ref[:, :k], tl) + nn(mlo_ref[:, :k], th))
            hi_out[:, ps], lo_out[:, ps] = split(s)
            if noise is not None:
                rr = r * n + lax.broadcasted_iota(jnp.int32, (n, PANEL), 0)
                cc = PANEL * p + lax.broadcasted_iota(jnp.int32, (n, PANEL), 1)
                factor_ref[:, ps] = jnp.where(rr >= cc, s, 0.0)

    @pl.when(step == 0)
    def _():
        tab_ref[...] = table()
        hhot_ref[...] = lookups(head_ref[:, f:], tab_ref[...])[1]
        rval_ref[...] = lookups(row_ref[:, f:], tab_ref[...])[0]
        solve(row_ref, rval_ref[...], noise_of(row_ref[:, f:]), rhi_ref, rlo_ref)

    value, hot = lookups(col_ref[:, f:], tab_ref[...])
    solve(col_ref, value, None, hi_ref, lo_ref)
    full = nt(row_ref[:, :f], col_ref[:, :f]) * nt(rval_ref[...], hot)
    ri = lax.broadcasted_iota(jnp.int32, (rows, tile), 0)
    li = step * tile + lax.broadcasted_iota(jnp.int32, (rows, tile), 1)
    col_local = li - r * rays
    full = full + jnp.where(ri - c * rays == col_local, jnp.where((col_local >= 0) & (col_local < rays), noise_of(row_ref[:, f:]), 0.0), 0.0)
    full = full - (nt(rhi_ref[...], hi_ref[...]) + (nt(rhi_ref[...], lo_ref[...]) + nt(rlo_ref[...], hi_ref[...])))
    first = jnp.where(r >= HEAD // rows, HEAD // (rows // rays * rays) * rays, tile * pl.num_programs(0))
    front_ref[:, 0, :] = jnp.where(li >= first, full, 0.0)


def front_and_factor(row, head, col, thi, tlo):
    rows, width = row.shape
    cols = col.shape[0]
    tile = 512
    whole = lambda a: pl.BlockSpec(a.shape, lambda i: (0,) * a.ndim)
    return pl.pallas_call(
        front_kernel,
        grid=(cols // tile,),
        out_shape=(jax.ShapeDtypeStruct((rows, 1, cols), F32), jax.ShapeDtypeStruct((rows, HEAD), F32)),
        in_specs=[whole(row), whole(head), pl.BlockSpec((tile, width), lambda i: (i, 0)), whole(thi), whole(tlo)],
        out_specs=(pl.BlockSpec((rows, 1, tile), lambda i: (0, 0, i)), pl.BlockSpec((rows, HEAD), lambda i: (0, 0))),
        scratch_shapes=[
            pltpu.VMEM((EXTRA, 512), BF16),
            pltpu.VMEM((HEAD, 256), BF16),
            pltpu.VMEM((rows, 256), BF16),
            pltpu.VMEM((rows, HEAD), BF16),
            pltpu.VMEM((rows, HEAD), BF16),
            pltpu.VMEM((tile, HEAD), BF16),
            pltpu.VMEM((tile, HEAD), BF16),
            pltpu.VMEM((max(tile, rows), HEAD), BF16),
            pltpu.VMEM((max(tile, rows), HEAD), BF16),
        ],
        compiler_params=pltpu.CompilerParams(vmem_limit_bytes=44 << 20),
        name="front_and_factor",
    )(row, head, col, thi, tlo)


def shards(features, slot_of_ray, noise):
    n_row, n_col = lax.axis_size("row"), lax.axis_size("col")
    rays = noise.shape[0]
    lanes = jnp.arange(EXTRA, dtype=jnp.int32)[None, :]
    hi = lax.reduce_precision(noise, 8, 7)
    mid = lax.reduce_precision(noise - hi, 8, 7)
    low = noise - hi - mid
    extra = jnp.where(lanes == slot_of_ray[:, None], 1.0, 0.0)
    for i, part in enumerate((hi, mid, low)):
        extra = jnp.where(lanes == NT + i, part[:, None], extra)
    payload = jnp.concatenate([features, extra.astype(BF16)], axis=1)
    width = payload.shape[1]
    col, row, head, *factors = gather_and_factor(payload, n_row, n_col)
    return front_and_factor(row.reshape(n_col * rays, width), head, col.reshape(n_row * rays, width), *factors)


def solution(mesh):
    return jax.shard_map(
        shards,
        mesh=mesh,
        in_specs=(P(("row", "col"), None), P(("row", "col")), P(("row", "col"))),
        out_specs=(P("row", "col", None), P("row", None)),
        check_vma=False,
    )
```

```python
import functools

import jax
import jax.numpy as jnp
from jax import lax
from jax.experimental import pallas as pl
from jax.experimental.pallas import tpu as pltpu
from jax.sharding import PartitionSpec as P

PANEL = 256
PANELS = 4
NT = 64
HEAD = PANEL * PANELS
EXTRA = 128
W = 8
B = 128
MESH = pl.DeviceIdType.MESH
HIGHEST = lax.Precision.HIGHEST
F32 = jnp.float32
BF16 = jnp.bfloat16
VMEM = pl.BlockSpec(memory_space=pltpu.VMEM)
ANY = pl.BlockSpec(memory_space=pl.ANY)


def time_rate():
    length = NT / 8.0
    return 1.0 / (2.0 * length * length)


def nn(a, b, precision=None):
    return lax.dot_general(a, b, (((1,), (0,)), ((), ())), precision=precision, preferred_element_type=F32)


def nt(a, b, precision=None):
    return lax.dot_general(a, b, (((1,), (1,)), ((), ())), precision=precision, preferred_element_type=F32)


def tn(a, b, precision=None):
    return lax.dot_general(a, b, (((0,), (0,)), ((), ())), precision=precision, preferred_element_type=F32)


def split(x):
    hi = x.astype(BF16)
    return hi, (x - hi.astype(F32)).astype(BF16)


NX, NZ = 4, 8
TRIANGLE = PANELS * (PANELS + 1) // 2


def remote(src, dst, send_sem, recv_sem, device):
    return pltpu.make_async_remote_copy(
        src_ref=src, dst_ref=dst, send_sem=send_sem, recv_sem=recv_sem, device_id=device, device_id_type=MESH
    )


class Feed:
    def __init__(self, n_row, n_col, pay_ref, head_ref, col_ref, row_ref, sems):
        self.n_row, self.n_col = n_row, n_col
        self.pay, self.head, self.col, self.row = pay_ref, head_ref, col_ref, row_ref
        (self.local, self.hsend, self.hrecv, self.csend, self.crecv, self.xsend, self.xrecv, self.rsend, self.rrecv) = sems
        self.r, self.c = lax.axis_index("row"), lax.axis_index("col")
        self.x, self.z = self.r // NZ, self.r % NZ
        self.ny = n_col // 2
        self.y, self.core = self.c // 2, self.c % 2
        self.rays = pay_ref.shape[0]
        self.part = self.rays // NX
        self.sends = []

    def at_row(self, x, z):
        return (x * NZ + z, self.c)

    def at_col(self, y, core):
        return (self.r, y * 2 + core)

    def announce(self):
        sem = pltpu.get_barrier_semaphore()
        for d in range(1, NX):
            pl.semaphore_signal(sem, inc=1, device_id=self.at_row((self.x + d) % NX, self.z), device_id_type=MESH)
        for d in range(1, NZ):
            pl.semaphore_signal(sem, inc=1, device_id=self.at_row(self.x, (self.z + d) % NZ), device_id_type=MESH)
        for d in range(1, self.n_col):
            pl.semaphore_signal(sem, inc=1, device_id=(self.r, (self.c + d) % self.n_col), device_id_type=MESH)

    def await_partners(self):
        pl.semaphore_wait(pltpu.get_barrier_semaphore(), NX + NZ + self.n_col - 3)

    def rows_of(self, q):
        return pl.ds(pl.multiple_of(q * self.part, self.part), self.part)

    def send(self, src, dst, recv, device, when=None):
        copy = remote(src, dst, self.hsend.at[len(self.sends)], self.hrecv.at[recv], device)
        self.sends.append((copy, when))
        if when is None:
            copy.start()
        else:
            pl.when(when)(copy.start)

    def arrived(self, dst, recv, when=None):
        copy = remote(dst, dst, self.hsend.at[0], self.hrecv.at[recv], (self.r, self.c))
        if when is None:
            copy.wait_recv()
        else:
            pl.when(when)(copy.wait_recv)

    def gather_head(self):
        x, y, z, core, ny = self.x, self.y, self.z, self.core, self.ny
        head = self.head
        x_first, y_first, y_then, x_then, other = 2, 2 + NX, 2 + NX + ny, 2 + NX + 2 * ny, 2 + 2 * NX + 2 * ny
        own = [head.at[b, core, y, self.rows_of(x)] for b in range(2)]
        for b in range(2):
            here = (x == 0) & (z == b)

            @pl.when(here)
            def _(b=b):
                head[b, core, y, 0 : self.part] = self.pay[0 : self.part]

            for q in range(1, NX):
                part = pl.ds(q * self.part, self.part)
                self.send(self.pay.at[part], head.at[b, core, y, part], b, self.at_row(q, z), here)
        for b in range(2):
            self.arrived(own[b], b, jnp.logical_not((x == 0) | (z != b)))
            for d in range(1, NZ):
                self.send(own[b], own[b], b, self.at_row(x, (z + d) % NZ), z == b)
        for b in range(2):
            self.arrived(own[b], b, z != b)
        for d in range(1, NX):
            self.send(own[0], own[0], x_first + x, self.at_row((x + d) % NX, z))
        for d in range(1, ny):
            self.send(own[1], own[1], y_first + y, self.at_col((y + d) % ny, core))
        self.start_columns()
        for d in range(1, NX):
            self.arrived(own[0], x_first + (x + d) % NX)
        block = head.at[0, core, y]
        for d in range(1, ny):
            self.send(block, block, y_then + y, self.at_col((y + d) % ny, core))
        for d in range(1, ny):
            self.arrived(own[1], y_first + (y + d) % ny)
        strip = head.at[1, core, :, self.rows_of(x)]
        for d in range(1, NX):
            self.send(strip, strip, x_then + x, self.at_row((x + d) % NX, z))
        for d in range(1, ny):
            self.arrived(block, y_then + (y + d) % ny)
        self.send(head.at[0, core], head.at[0, core], other, self.at_col(y, 1 - core))
        for d in range(1, NX):
            self.arrived(strip, x_then + (x + d) % NX)
        self.send(head.at[1, core], head.at[1, core], other + 1, self.at_col(y, 1 - core))
        for b in range(2):
            self.arrived(head.at[b, core], other + b)

    def column(self, z, d):
        return remote(
            self.pay, self.col.at[self.x * NZ + z], self.csend.at[d], self.crecv.at[z], self.at_row(self.x, (self.z + d) % NZ)
        )

    def plane(self, i):
        left, right = (self.x + NX - 1) % NX, (self.x + 1) % NX
        start, count = ((self.x * NZ, NZ), (self.x * NZ, NZ), (left * NZ, NZ // 2), (right * NZ + NZ // 2, NZ // 2))[i]
        where = self.col.at[pl.ds(start, count)]
        return remote(where, where, self.xsend.at[i], self.xrecv.at[i], self.at_row(left if i % 2 else right, self.z))

    def across_row(self, col, d):
        return remote(self.pay, self.row.at[col], self.rsend.at[d], self.rrecv.at[col], (self.r, (self.c + d) % self.n_col))

    def start_columns(self):
        self.own_col = pltpu.make_async_copy(self.pay, self.col.at[self.r], self.local.at[0])
        self.own_col.start()
        for d in range(1, NZ):
            self.column(self.z, d).start()

    def start_rows(self):
        self.own_row = pltpu.make_async_copy(self.pay, self.row.at[self.c], self.local.at[1])
        self.own_row.start()
        for d in range(1, self.n_col):
            self.across_row(self.c, d).start()

    def start_planes(self):
        self.own_col.wait()
        for d in range(1, NZ):
            self.column((self.z + d) % NZ, d).wait_recv()
        self.plane(0).start()
        self.plane(1).start()

    def relay_planes(self):
        for i in (0, 1):
            self.plane(i).wait_recv()
            self.plane(i + 2).start()

    def finish(self):
        self.own_row.wait()
        for d in range(1, self.n_col):
            self.across_row((self.c + d) % self.n_col, d).wait_recv()
        for i in (2, 3):
            self.plane(i).wait_recv()
        for copy, when in self.sends:
            if when is None:
                copy.wait_send()
            else:
                pl.when(when)(copy.wait_send)
        for d in range(1, NZ):
            self.column(self.z, d).wait_send()
        for i in range(4):
            self.plane(i).wait_send()
        for d in range(1, self.n_col):
            self.across_row(self.c, d).wait_send()


def table():
    s = lax.broadcasted_iota(jnp.int32, (EXTRA, 512), 0)
    q = lax.broadcasted_iota(jnp.int32, (EXTRA, 512), 1)
    part = q // NT
    gap = (s - q % NT).astype(F32)
    value = jnp.exp(-gap * gap * time_rate())
    hi = value.astype(BF16).astype(F32)
    mid = (value - hi).astype(BF16).astype(F32)
    low = value - hi - mid
    kernel_part = jnp.where(part == 0, hi, jnp.where(part == 1, mid, jnp.where(part == 2, low, 0.0)))
    chosen = jnp.where(part < 4, kernel_part, jnp.where(gap == 0.0, 1.0, 0.0))
    return jnp.where(s < NT, chosen, 0.0).astype(BF16)


def lookups(extra, tab):
    both = nn(extra, tab).astype(BF16)
    return both[:, :256], both[:, 256:]


def noise_of(extra):
    e = extra[:, NT : NT + 3].astype(F32)
    return (e[:, 0:1] + e[:, 1:2]) + e[:, 2:3]


def factor_block(d_ref, chores):
    lane = lax.broadcasted_iota(jnp.int32, (W, B), 1)
    sub = lax.broadcasted_iota(jnp.int32, (W, B), 0)

    def row(x, i):
        return jnp.broadcast_to(x[i : i + 1, :], (W, B))

    def col(x, i):
        return jnp.broadcast_to(x[:, i : i + 1], (W, B))

    steps = B // W
    for k in range(steps):
        lo = W * k
        rows = d_ref[lo : lo + W, :]
        work = [col(rows, lo + i) for i in range(W)]
        inside = (lane >= lo) & (lane < lo + W)
        work.append(jnp.where(inside, jnp.where(lane - lo == sub, 1.0, 0.0), rows))
        done = jnp.zeros((W, B), F32)
        for i in range(0, W, 2):
            first, second = work[i], work[i + 1]
            a, b, d = row(first, i), row(second, i), row(second, i + 1)
            det = a * d - b * b
            inverse = 1.0 / det
            for j in range(i + 2, W + 1):
                x0, x1 = row(work[j], i), row(work[j], i + 1)
                u0 = d * x0 - b * x1
                u1 = a * x1 - b * x0
                if j == W:
                    done = jnp.where(sub == i, x0 * lax.rsqrt(a), done)
                    done = jnp.where(sub == i + 1, u1 * (lax.rsqrt(a) * lax.rsqrt(det)), done)
                pivots = jnp.where(sub == i, u0, u1) * inverse
                others = work[j] - (first * u0 + second * u1) * inverse
                work[j] = jnp.where((sub == i) | (sub == i + 1), pivots, others)
        d_ref[lo : lo + W, :] = done
        spread = [row(work[W], i) for i in range(W)]
        for m in range(k + 1, steps):
            other = d_ref[W * m : W * m + W, :]
            terms = [col(other, lo + i) * spread[i] for i in range(W)]
            while len(terms) > 1:
                terms = [sum(terms[i : i + 2]) for i in range(0, len(terms), 2)]
            d_ref[W * m : W * m + W, :] = jnp.where(inside, 0.0, other) - terms[0]
        for chore in chores[len(chores) * k // steps : len(chores) * (k + 1) // steps]:
            chore()


def factor_head(head_ref, thi_ref, tlo_ref, s_ref, w_ref, t_ref, d_ref, hooks):
    n = HEAD // B
    f = head_ref.shape[1] - EXTRA
    extra = head_ref[:, f:]
    value, hot = lookups(extra, table())
    noise = noise_of(extra)

    def build(i):
        rs = slice(B * i, B * i + B)
        rr = lax.broadcasted_iota(jnp.int32, (B, HEAD - B * i), 0)
        cc = lax.broadcasted_iota(jnp.int32, (B, HEAD - B * i), 1)
        s_ref[rs, B * i :] = nt(head_ref[rs, :f], head_ref[B * i :, :f]) * nt(value[rs], hot[B * i :]) + jnp.where(rr == cc, noise[rs], 0.0)

    r = lax.broadcasted_iota(jnp.int32, (B, B), 0)
    c = lax.broadcasted_iota(jnp.int32, (B, B), 1)
    blk = lambda i: slice(B * i, B * i + B)

    def solve(j, i):
        solved = nn(w_ref[j], s_ref[blk(j), blk(i)], HIGHEST)
        s_ref[blk(j), blk(i)] = solved

    def update(j, i, m):
        s_ref[blk(i), blk(m)] -= tn(s_ref[blk(j), blk(i)], s_ref[blk(j), blk(m)], HIGHEST)

    pan = lambda p: slice(PANEL * p, PANEL * p + PANEL)
    spot = lambda p, q: p * (p + 1) // 2 + q

    def put(p, q, value):
        t_ref[spot(p, q)] = value
        thi_ref[spot(p, q)], tlo_ref[spot(p, q)] = split(value)

    def inverse_diagonal(p):
        a, b = w_ref[2 * p], w_ref[2 * p + 1]
        upper = -nt(tn(a, s_ref[blk(2 * p), blk(2 * p + 1)], HIGHEST), b, HIGHEST)
        zero = jnp.zeros((B, B), F32)
        put(p, p, jnp.concatenate([jnp.concatenate([a.T, upper], axis=1), jnp.concatenate([zero, b.T], axis=1)], axis=0))

    def inverse_sum(p, q):
        total = nn(t_ref[spot(q, q)], s_ref[pan(q), pan(p)], HIGHEST)
        for k in range(q + 1, p):
            total = total + nn(t_ref[spot(k, q)], s_ref[pan(k), pan(p)], HIGHEST)
        t_ref[spot(p, q)] = total

    def inverse_row(p, q):
        put(p, q, -nn(t_ref[spot(p, q)], t_ref[spot(p, p)], HIGHEST))

    build(0)
    chores = [functools.partial(build, i) for i in range(1, n)]
    for j in range(n):
        if j in hooks:
            hooks[j]()
        d_ref[...] = s_ref[blk(j), blk(j)]
        factor_block(d_ref, chores)
        w_ref[j] = jnp.where(r >= c, d_ref[...], 0.0)
        if j + 1 < n:
            solve(j, j + 1)
            update(j, j + 1, j + 1)
        chores = [functools.partial(solve, j, i) for i in range(j + 2, n)]
        chores += [functools.partial(update, j, i, m) for i in range(j + 1, n) for m in range(i, n) if m > j + 1]
        if j % 2:
            chores.append(functools.partial(inverse_diagonal, j // 2))
            chores += [functools.partial(inverse_row, j // 2, q) for q in range(j // 2)]
        elif j:
            chores += [functools.partial(inverse_sum, j // 2, q) for q in range(j // 2)]
    for chore in chores:
        chore()


def fill_payload(feat_ref, slot_ref, noise_ref, pay_ref):
    rays, f = feat_ref.shape
    lane = lax.broadcasted_iota(jnp.int32, (EXTRA, rays), 0)
    noise = noise_ref[...]
    hi = noise.astype(BF16).astype(F32)
    mid = (noise - hi).astype(BF16).astype(F32)
    extra = jnp.where(lane == slot_ref[...], 1.0, 0.0)
    for i, part in enumerate((hi, mid, noise - hi - mid)):
        extra = jnp.where(lane == NT + i, part, extra)
    pay_ref[:, :f] = feat_ref[...]
    pay_ref[:, f:] = extra.T.astype(BF16)


def head_kernel(n_row, n_col, feat_ref, slot_ref, noise_ref, col_ref, row_ref, out_head_ref, thi_ref, tlo_ref, pay_ref, blocks_ref, head_ref, s_ref, w_ref, t_ref, d_ref, *sems):
    feed = Feed(n_row, n_col, pay_ref, blocks_ref, col_ref, row_ref, sems)
    feed.announce()
    fill_payload(feat_ref, slot_ref, noise_ref, pay_ref)
    feed.await_partners()
    feed.gather_head()

    def start_planes_and_rows():
        feed.start_planes()
        feed.start_rows()

    rays = feed.rays
    for i in range(HEAD // rays):
        head_ref[i * rays : i * rays + rays, :] = blocks_ref[i // n_col, i % 2, i % n_col // 2]
    out = pltpu.make_async_copy(head_ref, out_head_ref, feed.local.at[2])
    out.start()
    factor_head(head_ref, thi_ref, tlo_ref, s_ref, w_ref, t_ref, d_ref, {1: start_planes_and_rows, 6: feed.relay_planes})
    feed.finish()
    out.wait()


def gather_and_factor(features, slots, noise, n_row, n_col):
    rays, width = features.shape[0], features.shape[1] + EXTRA
    dma = pltpu.SemaphoreType.DMA
    return pl.pallas_call(
        functools.partial(head_kernel, n_row, n_col),
        out_shape=(
            jax.ShapeDtypeStruct((n_row, rays, width), BF16),
            jax.ShapeDtypeStruct((n_col, rays, width), BF16),
            jax.ShapeDtypeStruct((HEAD, width), BF16),
            jax.ShapeDtypeStruct((TRIANGLE, PANEL, PANEL), BF16),
            jax.ShapeDtypeStruct((TRIANGLE, PANEL, PANEL), BF16),
        ),
        in_specs=[VMEM, VMEM, VMEM],
        out_specs=(ANY, ANY, ANY, VMEM, VMEM),
        scratch_shapes=[
            pltpu.VMEM((rays, width), BF16),
            pltpu.VMEM((2, 2, n_col // 2, rays, width), BF16),
            pltpu.VMEM((HEAD, width), BF16),
            pltpu.VMEM((HEAD, HEAD), F32),
            pltpu.VMEM((HEAD // B, B, B), F32),
            pltpu.VMEM((TRIANGLE, PANEL, PANEL), F32),
            pltpu.VMEM((B, B), F32),
            dma((3,)), dma((48,)), dma((32,)), dma((NZ,)), dma((NZ,)), dma((4,)), dma((4,)), dma((n_col,)), dma((n_col,)),
        ],
        compiler_params=pltpu.CompilerParams(collective_id=0, has_side_effects=True, vmem_limit_bytes=40 << 20),
        name="gather_and_factor",
    )(features, slots, noise)


def front_kernel(row_ref, head_ref, col_ref, thi_ref, tlo_ref, front_ref, factor_ref, tab_ref, hhot_ref, rval_ref, rhi_ref, rlo_ref, hi_ref, lo_ref, mhi_ref, mlo_ref):
    step = pl.program_id(0)
    r, c = lax.axis_index("row"), lax.axis_index("col")
    f = head_ref.shape[1] - EXTRA
    rows = row_ref.shape[0]
    tile = col_ref.shape[0]
    rays = rows // lax.axis_size("col")

    def solve(ref, value, noise, hi_out, lo_out):
        feat = ref[:, :f]
        n = ref.shape[0]
        for p in range(PANELS):
            ps = slice(PANEL * p, PANEL * p + PANEL)
            x = nt(feat, head_ref[ps, :f]) * nt(value, hhot_ref[ps])
            if noise is not None:
                rr = r * n + lax.broadcasted_iota(jnp.int32, (n, PANEL), 0)
                cc = PANEL * p + lax.broadcasted_iota(jnp.int32, (n, PANEL), 1)
                x = x + jnp.where(rr == cc, noise, 0.0)
            mhi_ref[:, ps], mlo_ref[:, ps] = split(x)
        for p in range(PANELS):
            ps = slice(PANEL * p, PANEL * p + PANEL)
            k = PANEL * (p + 1)
            at = p * (p + 1) // 2
            th, tl = thi_ref[at : at + p + 1].reshape(k, PANEL), tlo_ref[at : at + p + 1].reshape(k, PANEL)
            s = nn(mhi_ref[:, :k], th) + (nn(mhi_ref[:, :k], tl) + nn(mlo_ref[:, :k], th))
            hi_out[:, ps], lo_out[:, ps] = split(s)
            if noise is not None:
                rr = r * n + lax.broadcasted_iota(jnp.int32, (n, PANEL), 0)
                cc = PANEL * p + lax.broadcasted_iota(jnp.int32, (n, PANEL), 1)
                factor_ref[:, ps] = jnp.where(rr >= cc, s, 0.0)

    @pl.when(step == 0)
    def _():
        tab_ref[...] = table()
        hhot_ref[...] = lookups(head_ref[:, f:], tab_ref[...])[1]
        rval_ref[...] = lookups(row_ref[:, f:], tab_ref[...])[0]
        solve(row_ref, rval_ref[...], noise_of(row_ref[:, f:]), rhi_ref, rlo_ref)

    value, hot = lookups(col_ref[:, f:], tab_ref[...])
    solve(col_ref, value, None, hi_ref, lo_ref)
    full = nt(row_ref[:, :f], col_ref[:, :f]) * nt(rval_ref[...], hot)
    ri = lax.broadcasted_iota(jnp.int32, (rows, tile), 0)
    li = step * tile + lax.broadcasted_iota(jnp.int32, (rows, tile), 1)
    col_local = li - r * rays
    full = full + jnp.where(ri - c * rays == col_local, jnp.where((col_local >= 0) & (col_local < rays), noise_of(row_ref[:, f:]), 0.0), 0.0)
    full = full - (nt(rhi_ref[...], hi_ref[...]) + (nt(rhi_ref[...], lo_ref[...]) + nt(rlo_ref[...], hi_ref[...])))
    first = jnp.where(r >= HEAD // rows, HEAD // (rows // rays * rays) * rays, tile * pl.num_programs(0))
    front_ref[:, 0, :] = jnp.where(li >= first, full, 0.0)


def front_and_factor(row, head, col, thi, tlo):
    rows, width = row.shape
    cols = col.shape[0]
    tile = 512
    whole = lambda a: pl.BlockSpec(a.shape, lambda i: (0,) * a.ndim)
    return pl.pallas_call(
        front_kernel,
        grid=(cols // tile,),
        out_shape=(jax.ShapeDtypeStruct((rows, 1, cols), F32), jax.ShapeDtypeStruct((rows, HEAD), F32)),
        in_specs=[whole(row), whole(head), pl.BlockSpec((tile, width), lambda i: (i, 0)), whole(thi), whole(tlo)],
        out_specs=(pl.BlockSpec((rows, 1, tile), lambda i: (0, 0, i)), pl.BlockSpec((rows, HEAD), lambda i: (0, 0))),
        scratch_shapes=[
            pltpu.VMEM((EXTRA, 512), BF16),
            pltpu.VMEM((HEAD, 256), BF16),
            pltpu.VMEM((rows, 256), BF16),
            pltpu.VMEM((rows, HEAD), BF16),
            pltpu.VMEM((rows, HEAD), BF16),
            pltpu.VMEM((tile, HEAD), BF16),
            pltpu.VMEM((tile, HEAD), BF16),
            pltpu.VMEM((max(tile, rows), HEAD), BF16),
            pltpu.VMEM((max(tile, rows), HEAD), BF16),
        ],
        compiler_params=pltpu.CompilerParams(vmem_limit_bytes=44 << 20),
        name="front_and_factor",
    )(row, head, col, thi, tlo)


def shards(features, slot_of_ray, noise):
    n_row, n_col = lax.axis_size("row"), lax.axis_size("col")
    rays = noise.shape[0]
    width = features.shape[1] + EXTRA
    col, row, head, *factors = gather_and_factor(features, slot_of_ray[None, :], noise[None, :], n_row, n_col)
    return front_and_factor(row.reshape(n_col * rays, width), head, col.reshape(n_row * rays, width), *factors)


def solution(mesh):
    return jax.shard_map(
        shards,
        mesh=mesh,
        in_specs=(P(("row", "col"), None), P(("row", "col")), P(("row", "col"))),
        out_specs=(P("row", "col", None), P("row", None)),
        check_vma=False,
    )
```

```python
import functools

import jax
import jax.numpy as jnp
from jax import lax
from jax.experimental import pallas as pl
from jax.experimental.pallas import tpu as pltpu
from jax.sharding import PartitionSpec as P

PANEL = 256
PANELS = 4
NT = 64
HEAD = PANEL * PANELS
EXTRA = 128
W = 8
B = 128
MESH = pl.DeviceIdType.MESH
HIGHEST = lax.Precision.HIGHEST
F32 = jnp.float32
BF16 = jnp.bfloat16
VMEM = pl.BlockSpec(memory_space=pltpu.VMEM)
ANY = pl.BlockSpec(memory_space=pl.ANY)


def time_rate():
    length = NT / 8.0
    return 1.0 / (2.0 * length * length)


def nn(a, b, precision=None):
    return lax.dot_general(a, b, (((1,), (0,)), ((), ())), precision=precision, preferred_element_type=F32)


def nt(a, b, precision=None):
    return lax.dot_general(a, b, (((1,), (1,)), ((), ())), precision=precision, preferred_element_type=F32)


def tn(a, b, precision=None):
    return lax.dot_general(a, b, (((0,), (0,)), ((), ())), precision=precision, preferred_element_type=F32)


def split(x):
    hi = x.astype(BF16)
    return hi, (x - hi.astype(F32)).astype(BF16)


NX, NZ = 4, 8
TRIANGLE = PANELS * (PANELS + 1) // 2


def remote(src, dst, send_sem, recv_sem, device):
    return pltpu.make_async_remote_copy(
        src_ref=src, dst_ref=dst, send_sem=send_sem, recv_sem=recv_sem, device_id=device, device_id_type=MESH
    )


class Feed:
    def __init__(self, n_row, n_col, pay_ref, head_ref, col_ref, row_ref, sems):
        self.n_row, self.n_col = n_row, n_col
        self.pay, self.head, self.col, self.row = pay_ref, head_ref, col_ref, row_ref
        (self.local, self.hsend, self.hrecv, self.csend, self.crecv, self.xsend, self.xrecv, self.rsend, self.rrecv) = sems
        self.r, self.c = lax.axis_index("row"), lax.axis_index("col")
        self.x, self.z = self.r // NZ, self.r % NZ
        self.ny = n_col // 2
        self.y, self.core = self.c // 2, self.c % 2
        self.rays = pay_ref.shape[0]
        self.part = self.rays // NX
        self.sends = []

    def at_row(self, x, z):
        return (x * NZ + z, self.c)

    def at_col(self, y, core):
        return (self.r, y * 2 + core)

    def announce(self):
        sem = pltpu.get_barrier_semaphore()
        for d in range(1, NX):
            pl.semaphore_signal(sem, inc=1, device_id=self.at_row((self.x + d) % NX, self.z), device_id_type=MESH)
        for d in range(1, NZ):
            pl.semaphore_signal(sem, inc=1, device_id=self.at_row(self.x, (self.z + d) % NZ), device_id_type=MESH)
        for d in range(1, self.n_col):
            pl.semaphore_signal(sem, inc=1, device_id=(self.r, (self.c + d) % self.n_col), device_id_type=MESH)

    def await_partners(self):
        pl.semaphore_wait(pltpu.get_barrier_semaphore(), NX + NZ + self.n_col - 3)

    def rows_of(self, q):
        return pl.ds(pl.multiple_of(q * self.part, self.part), self.part)

    def send(self, src, dst, recv, device, when=None):
        copy = remote(src, dst, self.hsend.at[len(self.sends)], self.hrecv.at[recv], device)
        self.sends.append((copy, when))
        if when is None:
            copy.start()
        else:
            pl.when(when)(copy.start)

    def arrived(self, dst, recv, when=None):
        copy = remote(dst, dst, self.hsend.at[0], self.hrecv.at[recv], (self.r, self.c))
        if when is None:
            copy.wait_recv()
        else:
            pl.when(when)(copy.wait_recv)

    def gather_head(self):
        x, y, z, core, ny = self.x, self.y, self.z, self.core, self.ny
        head = self.head
        x_first, y_first, y_then, x_then, other = 2, 2 + NX, 2 + NX + ny, 2 + NX + 2 * ny, 2 + 2 * NX + 2 * ny
        own = [head.at[b, core, y, self.rows_of(x)] for b in range(2)]
        for b in range(2):
            here = (x == 0) & (z == b)

            @pl.when(here)
            def _(b=b):
                head[b, core, y, 0 : self.part] = self.pay[0 : self.part]

            for q in range(1, NX):
                part = pl.ds(q * self.part, self.part)
                self.send(self.pay.at[part], head.at[b, core, y, part], b, self.at_row(q, z), here)
        for b in range(2):
            self.arrived(own[b], b, jnp.logical_not((x == 0) | (z != b)))
            for d in range(1, NZ):
                self.send(own[b], own[b], b, self.at_row(x, (z + d) % NZ), z == b)
        for b in range(2):
            self.arrived(own[b], b, z != b)
        for d in range(1, NX):
            self.send(own[0], own[0], x_first + x, self.at_row((x + d) % NX, z))
        for d in range(1, ny):
            self.send(own[1], own[1], y_first + y, self.at_col((y + d) % ny, core))
        for d in range(1, NX):
            self.arrived(own[0], x_first + (x + d) % NX)
        block = head.at[0, core, y]
        for d in range(1, ny):
            self.send(block, block, y_then + y, self.at_col((y + d) % ny, core))
        for d in range(1, ny):
            self.arrived(own[1], y_first + (y + d) % ny)
        strip = head.at[1, core, :, self.rows_of(x)]
        for d in range(1, NX):
            self.send(strip, strip, x_then + x, self.at_row((x + d) % NX, z))
        self.start_columns()
        for d in range(1, ny):
            self.arrived(block, y_then + (y + d) % ny)
        self.send(head.at[0, core], head.at[0, core], other, self.at_col(y, 1 - core))
        for d in range(1, NX):
            self.arrived(strip, x_then + (x + d) % NX)
        self.send(head.at[1, core], head.at[1, core], other + 1, self.at_col(y, 1 - core))
        for b in range(2):
            self.arrived(head.at[b, core], other + b)

    def column(self, z, d):
        return remote(
            self.pay, self.col.at[self.x * NZ + z], self.csend.at[d], self.crecv.at[z], self.at_row(self.x, (self.z + d) % NZ)
        )

    def plane(self, i):
        left, right = (self.x + NX - 1) % NX, (self.x + 1) % NX
        start, count = ((self.x * NZ, NZ), (self.x * NZ, NZ), (left * NZ, NZ // 2), (right * NZ + NZ // 2, NZ // 2))[i]
        where = self.col.at[pl.ds(start, count)]
        return remote(where, where, self.xsend.at[i], self.xrecv.at[i], self.at_row(left if i % 2 else right, self.z))

    def across_row(self, col, d):
        return remote(self.pay, self.row.at[col], self.rsend.at[d], self.rrecv.at[col], (self.r, (self.c + d) % self.n_col))

    def start_columns(self):
        self.own_col = pltpu.make_async_copy(self.pay, self.col.at[self.r], self.local.at[0])
        self.own_col.start()
        for d in range(1, NZ):
            self.column(self.z, d).start()

    def start_rows(self):
        self.own_row = pltpu.make_async_copy(self.pay, self.row.at[self.c], self.local.at[1])
        self.own_row.start()
        for d in range(1, self.n_col):
            self.across_row(self.c, d).start()

    def start_planes(self):
        self.own_col.wait()
        for d in range(1, NZ):
            self.column((self.z + d) % NZ, d).wait_recv()
        self.plane(0).start()
        self.plane(1).start()

    def relay_planes(self):
        for i in (0, 1):
            self.plane(i).wait_recv()
            self.plane(i + 2).start()

    def finish(self):
        self.own_row.wait()
        for d in range(1, self.n_col):
            self.across_row((self.c + d) % self.n_col, d).wait_recv()
        for i in (2, 3):
            self.plane(i).wait_recv()
        for copy, when in self.sends:
            if when is None:
                copy.wait_send()
            else:
                pl.when(when)(copy.wait_send)
        for d in range(1, NZ):
            self.column(self.z, d).wait_send()
        for i in range(4):
            self.plane(i).wait_send()
        for d in range(1, self.n_col):
            self.across_row(self.c, d).wait_send()


def table():
    s = lax.broadcasted_iota(jnp.int32, (EXTRA, 512), 0)
    q = lax.broadcasted_iota(jnp.int32, (EXTRA, 512), 1)
    part = q // NT
    gap = (s - q % NT).astype(F32)
    value = jnp.exp(-gap * gap * time_rate())
    hi = value.astype(BF16).astype(F32)
    mid = (value - hi).astype(BF16).astype(F32)
    low = value - hi - mid
    kernel_part = jnp.where(part == 0, hi, jnp.where(part == 1, mid, jnp.where(part == 2, low, 0.0)))
    chosen = jnp.where(part < 4, kernel_part, jnp.where(gap == 0.0, 1.0, 0.0))
    return jnp.where(s < NT, chosen, 0.0).astype(BF16)


def lookups(extra, tab):
    both = nn(extra, tab).astype(BF16)
    return both[:, :256], both[:, 256:]


def noise_of(extra):
    e = extra[:, NT : NT + 3].astype(F32)
    return (e[:, 0:1] + e[:, 1:2]) + e[:, 2:3]


def factor_block(d_ref, chores):
    lane = lax.broadcasted_iota(jnp.int32, (W, B), 1)
    sub = lax.broadcasted_iota(jnp.int32, (W, B), 0)

    def row(x, i):
        return jnp.broadcast_to(x[i : i + 1, :], (W, B))

    def col(x, i):
        return jnp.broadcast_to(x[:, i : i + 1], (W, B))

    steps = B // W
    for k in range(steps):
        lo = W * k
        rows = d_ref[lo : lo + W, :]
        work = [col(rows, lo + i) for i in range(W)]
        inside = (lane >= lo) & (lane < lo + W)
        work.append(jnp.where(inside, jnp.where(lane - lo == sub, 1.0, 0.0), rows))
        done = jnp.zeros((W, B), F32)
        for i in range(0, W, 2):
            first, second = work[i], work[i + 1]
            a, b, d = row(first, i), row(second, i), row(second, i + 1)
            det = a * d - b * b
            inverse = 1.0 / det
            for j in range(i + 2, W + 1):
                x0, x1 = row(work[j], i), row(work[j], i + 1)
                u0 = d * x0 - b * x1
                u1 = a * x1 - b * x0
                if j == W:
                    done = jnp.where(sub == i, x0 * lax.rsqrt(a), done)
                    done = jnp.where(sub == i + 1, u1 * (lax.rsqrt(a) * lax.rsqrt(det)), done)
                pivots = jnp.where(sub == i, u0, u1) * inverse
                others = work[j] - (first * u0 + second * u1) * inverse
                work[j] = jnp.where((sub == i) | (sub == i + 1), pivots, others)
        d_ref[lo : lo + W, :] = done
        spread = [row(work[W], i) for i in range(W)]
        for m in range(k + 1, steps):
            other = d_ref[W * m : W * m + W, :]
            terms = [col(other, lo + i) * spread[i] for i in range(W)]
            while len(terms) > 1:
                terms = [sum(terms[i : i + 2]) for i in range(0, len(terms), 2)]
            d_ref[W * m : W * m + W, :] = jnp.where(inside, 0.0, other) - terms[0]
        for chore in chores[len(chores) * k // steps : len(chores) * (k + 1) // steps]:
            chore()


def factor_head(head_ref, thi_ref, tlo_ref, s_ref, w_ref, t_ref, d_ref, hooks):
    n = HEAD // B
    f = head_ref.shape[1] - EXTRA
    extra = head_ref[:, f:]
    value, hot = lookups(extra, table())
    noise = noise_of(extra)

    def build(i):
        rs = slice(B * i, B * i + B)
        rr = lax.broadcasted_iota(jnp.int32, (B, HEAD - B * i), 0)
        cc = lax.broadcasted_iota(jnp.int32, (B, HEAD - B * i), 1)
        s_ref[rs, B * i :] = nt(head_ref[rs, :f], head_ref[B * i :, :f]) * nt(value[rs], hot[B * i :]) + jnp.where(rr == cc, noise[rs], 0.0)

    r = lax.broadcasted_iota(jnp.int32, (B, B), 0)
    c = lax.broadcasted_iota(jnp.int32, (B, B), 1)
    blk = lambda i: slice(B * i, B * i + B)

    def solve(j, i):
        solved = nn(w_ref[j], s_ref[blk(j), blk(i)], HIGHEST)
        s_ref[blk(j), blk(i)] = solved

    def update(j, i, m):
        s_ref[blk(i), blk(m)] -= tn(s_ref[blk(j), blk(i)], s_ref[blk(j), blk(m)], HIGHEST)

    pan = lambda p: slice(PANEL * p, PANEL * p + PANEL)
    spot = lambda p, q: p * (p + 1) // 2 + q

    def put(p, q, value):
        t_ref[spot(p, q)] = value
        thi_ref[spot(p, q)], tlo_ref[spot(p, q)] = split(value)

    def inverse_diagonal(p):
        a, b = w_ref[2 * p], w_ref[2 * p + 1]
        upper = -nt(tn(a, s_ref[blk(2 * p), blk(2 * p + 1)], HIGHEST), b, HIGHEST)
        zero = jnp.zeros((B, B), F32)
        put(p, p, jnp.concatenate([jnp.concatenate([a.T, upper], axis=1), jnp.concatenate([zero, b.T], axis=1)], axis=0))

    def inverse_sum(p, q):
        total = nn(t_ref[spot(q, q)], s_ref[pan(q), pan(p)], HIGHEST)
        for k in range(q + 1, p):
            total = total + nn(t_ref[spot(k, q)], s_ref[pan(k), pan(p)], HIGHEST)
        t_ref[spot(p, q)] = total

    def inverse_row(p, q):
        put(p, q, -nn(t_ref[spot(p, q)], t_ref[spot(p, p)], HIGHEST))

    build(0)
    chores = [functools.partial(build, i) for i in range(1, n)]
    for j in range(n):
        if j in hooks:
            hooks[j]()
        d_ref[...] = s_ref[blk(j), blk(j)]
        factor_block(d_ref, chores)
        w_ref[j] = jnp.where(r >= c, d_ref[...], 0.0)
        if j + 1 < n:
            solve(j, j + 1)
            update(j, j + 1, j + 1)
        chores = [functools.partial(solve, j, i) for i in range(j + 2, n)]
        chores += [functools.partial(update, j, i, m) for i in range(j + 1, n) for m in range(i, n) if m > j + 1]
        if j % 2:
            chores.append(functools.partial(inverse_diagonal, j // 2))
            chores += [functools.partial(inverse_row, j // 2, q) for q in range(j // 2)]
        elif j:
            chores += [functools.partial(inverse_sum, j // 2, q) for q in range(j // 2)]
    for chore in chores:
        chore()


def fill_payload(feat_ref, slot_ref, noise_ref, pay_ref):
    rays, f = feat_ref.shape
    lane = lax.broadcasted_iota(jnp.int32, (EXTRA, rays), 0)
    noise = noise_ref[...]
    hi = noise.astype(BF16).astype(F32)
    mid = (noise - hi).astype(BF16).astype(F32)
    extra = jnp.where(lane == slot_ref[...], 1.0, 0.0)
    for i, part in enumerate((hi, mid, noise - hi - mid)):
        extra = jnp.where(lane == NT + i, part, extra)
    pay_ref[:, :f] = feat_ref[...]
    pay_ref[:, f:] = extra.T.astype(BF16)


def head_kernel(n_row, n_col, feat_ref, slot_ref, noise_ref, col_ref, row_ref, out_head_ref, thi_ref, tlo_ref, pay_ref, blocks_ref, head_ref, s_ref, w_ref, t_ref, d_ref, *sems):
    feed = Feed(n_row, n_col, pay_ref, blocks_ref, col_ref, row_ref, sems)
    feed.announce()
    fill_payload(feat_ref, slot_ref, noise_ref, pay_ref)
    feed.await_partners()
    feed.gather_head()

    def start_planes_and_rows():
        feed.start_planes()
        feed.start_rows()

    rays = feed.rays
    for i in range(HEAD // rays):
        head_ref[i * rays : i * rays + rays, :] = blocks_ref[i // n_col, i % 2, i % n_col // 2]
    out = pltpu.make_async_copy(head_ref, out_head_ref, feed.local.at[2])
    out.start()
    factor_head(head_ref, thi_ref, tlo_ref, s_ref, w_ref, t_ref, d_ref, {2: start_planes_and_rows, 6: feed.relay_planes})
    feed.finish()
    out.wait()


def gather_and_factor(features, slots, noise, n_row, n_col):
    rays, width = features.shape[0], features.shape[1] + EXTRA
    dma = pltpu.SemaphoreType.DMA
    return pl.pallas_call(
        functools.partial(head_kernel, n_row, n_col),
        out_shape=(
            jax.ShapeDtypeStruct((n_row, rays, width), BF16),
            jax.ShapeDtypeStruct((n_col, rays, width), BF16),
            jax.ShapeDtypeStruct((HEAD, width), BF16),
            jax.ShapeDtypeStruct((TRIANGLE, PANEL, PANEL), BF16),
            jax.ShapeDtypeStruct((TRIANGLE, PANEL, PANEL), BF16),
        ),
        in_specs=[VMEM, VMEM, VMEM],
        out_specs=(ANY, ANY, ANY, VMEM, VMEM),
        scratch_shapes=[
            pltpu.VMEM((rays, width), BF16),
            pltpu.VMEM((2, 2, n_col // 2, rays, width), BF16),
            pltpu.VMEM((HEAD, width), BF16),
            pltpu.VMEM((HEAD, HEAD), F32),
            pltpu.VMEM((HEAD // B, B, B), F32),
            pltpu.VMEM((TRIANGLE, PANEL, PANEL), F32),
            pltpu.VMEM((B, B), F32),
            dma((3,)), dma((48,)), dma((32,)), dma((NZ,)), dma((NZ,)), dma((4,)), dma((4,)), dma((n_col,)), dma((n_col,)),
        ],
        compiler_params=pltpu.CompilerParams(collective_id=0, has_side_effects=True, vmem_limit_bytes=40 << 20),
        name="gather_and_factor",
    )(features, slots, noise)


def front_kernel(row_ref, head_ref, col_ref, thi_ref, tlo_ref, front_ref, factor_ref, tab_ref, hhot_ref, rval_ref, rhi_ref, rlo_ref, hi_ref, lo_ref, mhi_ref, mlo_ref):
    step = pl.program_id(0)
    r, c = lax.axis_index("row"), lax.axis_index("col")
    f = head_ref.shape[1] - EXTRA
    rows = row_ref.shape[0]
    tile = col_ref.shape[0]
    rays = rows // lax.axis_size("col")

    def solve(ref, value, noise, hi_out, lo_out):
        feat = ref[:, :f]
        n = ref.shape[0]
        for p in range(PANELS):
            ps = slice(PANEL * p, PANEL * p + PANEL)
            x = nt(feat, head_ref[ps, :f]) * nt(value, hhot_ref[ps])
            if noise is not None:
                rr = r * n + lax.broadcasted_iota(jnp.int32, (n, PANEL), 0)
                cc = PANEL * p + lax.broadcasted_iota(jnp.int32, (n, PANEL), 1)
                x = x + jnp.where(rr == cc, noise, 0.0)
            mhi_ref[:, ps], mlo_ref[:, ps] = split(x)
        for p in range(PANELS):
            ps = slice(PANEL * p, PANEL * p + PANEL)
            k = PANEL * (p + 1)
            at = p * (p + 1) // 2
            th, tl = thi_ref[at : at + p + 1].reshape(k, PANEL), tlo_ref[at : at + p + 1].reshape(k, PANEL)
            s = nn(mhi_ref[:, :k], th) + (nn(mhi_ref[:, :k], tl) + nn(mlo_ref[:, :k], th))
            hi_out[:, ps], lo_out[:, ps] = split(s)
            if noise is not None:
                rr = r * n + lax.broadcasted_iota(jnp.int32, (n, PANEL), 0)
                cc = PANEL * p + lax.broadcasted_iota(jnp.int32, (n, PANEL), 1)
                factor_ref[:, ps] = jnp.where(rr >= cc, s, 0.0)

    @pl.when(step == 0)
    def _():
        tab_ref[...] = table()
        hhot_ref[...] = lookups(head_ref[:, f:], tab_ref[...])[1]
        rval_ref[...] = lookups(row_ref[:, f:], tab_ref[...])[0]
        solve(row_ref, rval_ref[...], noise_of(row_ref[:, f:]), rhi_ref, rlo_ref)

    value, hot = lookups(col_ref[:, f:], tab_ref[...])
    solve(col_ref, value, None, hi_ref, lo_ref)
    full = nt(row_ref[:, :f], col_ref[:, :f]) * nt(rval_ref[...], hot)
    ri = lax.broadcasted_iota(jnp.int32, (rows, tile), 0)
    li = step * tile + lax.broadcasted_iota(jnp.int32, (rows, tile), 1)
    col_local = li - r * rays
    full = full + jnp.where(ri - c * rays == col_local, jnp.where((col_local >= 0) & (col_local < rays), noise_of(row_ref[:, f:]), 0.0), 0.0)
    full = full - (nt(rhi_ref[...], hi_ref[...]) + (nt(rhi_ref[...], lo_ref[...]) + nt(rlo_ref[...], hi_ref[...])))
    first = jnp.where(r >= HEAD // rows, HEAD // (rows // rays * rays) * rays, tile * pl.num_programs(0))
    front_ref[:, 0, :] = jnp.where(li >= first, full, 0.0)


def front_and_factor(row, head, col, thi, tlo):
    rows, width = row.shape
    cols = col.shape[0]
    tile = 512
    whole = lambda a: pl.BlockSpec(a.shape, lambda i: (0,) * a.ndim)
    return pl.pallas_call(
        front_kernel,
        grid=(cols // tile,),
        out_shape=(jax.ShapeDtypeStruct((rows, 1, cols), F32), jax.ShapeDtypeStruct((rows, HEAD), F32)),
        in_specs=[whole(row), whole(head), pl.BlockSpec((tile, width), lambda i: (i, 0)), whole(thi), whole(tlo)],
        out_specs=(pl.BlockSpec((rows, 1, tile), lambda i: (0, 0, i)), pl.BlockSpec((rows, HEAD), lambda i: (0, 0))),
        scratch_shapes=[
            pltpu.VMEM((EXTRA, 512), BF16),
            pltpu.VMEM((HEAD, 256), BF16),
            pltpu.VMEM((rows, 256), BF16),
            pltpu.VMEM((rows, HEAD), BF16),
            pltpu.VMEM((rows, HEAD), BF16),
            pltpu.VMEM((tile, HEAD), BF16),
            pltpu.VMEM((tile, HEAD), BF16),
            pltpu.VMEM((max(tile, rows), HEAD), BF16),
            pltpu.VMEM((max(tile, rows), HEAD), BF16),
        ],
        compiler_params=pltpu.CompilerParams(vmem_limit_bytes=44 << 20),
        name="front_and_factor",
    )(row, head, col, thi, tlo)


def shards(features, slot_of_ray, noise):
    n_row, n_col = lax.axis_size("row"), lax.axis_size("col")
    rays = noise.shape[0]
    width = features.shape[1] + EXTRA
    col, row, head, *factors = gather_and_factor(features, slot_of_ray[None, :], noise[None, :], n_row, n_col)
    return front_and_factor(row.reshape(n_col * rays, width), head, col.reshape(n_row * rays, width), *factors)


def solution(mesh):
    return jax.shard_map(
        shards,
        mesh=mesh,
        in_specs=(P(("row", "col"), None), P(("row", "col")), P(("row", "col"))),
        out_specs=(P("row", "col", None), P("row", None)),
        check_vma=False,
    )
```
